32 devices in a mesh: row: 8 (over z, core), col: 4 (over y, x).
Axes of the slice: x: 2, y: 2, z: 4, core: 2. Of those that a mesh axis runs over, the one named last changes fastest.
Arguments:
- curve_embed: bfloat16 [2048, 128], P(('row', 'col')), may hold values from -6 to 6
- solution: float32 [2048, 256], P(('row', 'col')), may hold values from -0.5 to 0.5
- targets: bfloat16 [2048, 256], P(('row', 'col')), may hold values from -6 to 6
- lengths: int32 [2048], P(('row', 'col')), may hold values from 1 to 256
- slot_curve: int32 [2048], P(('row', 'col')), may hold values from 0 to 2047, as said below
- epoch_kernel: float32 [256, 256], replicated, as said below
Outputs:
- row_grad: float32 [2048, 128], P(('row', 'col'))
- col_grad: float32 [2048, 128], P(('row', 'col'))
The draws below stay inside these ranges and needn't reach their ends.
Inputs may be any that keep to these rules, and one draw needn't show every extreme that they name: Within each aligned group of 256 slots, slot_curve is a permutation of that group's own slot numbers. `epoch_kernel`: symmetric positive definite.
All inputs are finite; a program needn't handle non-finite values.
Results may differ from the reference program's by a relative error of at most 0.0036.
Values may be sent and summed in bfloat16 or wider, within the bound.
No kernel may reach another device: no remote copies, remote signals or barrier semaphores. Data moves between devices by JAX's collectives and lax.ppermute only.
A program may use at most 64 MiB of HBM per device.

```python
import math
from functools import partial
import jax
import jax.numpy as jnp
from jax import lax

D = 128
E = 256
NCURVES = 2048
GROUP = 256


def draw_curve_embed(key, part):
    clusters = max(1, min(64, NCURVES // 16))
    base_key = jax.random.fold_in(key, 37)
    subkeys = jax.random.split(base_key, 5)
    member = jax.random.randint(subkeys[0], (NCURVES,), 0, clusters).astype(jnp.int32)
    spread = jax.random.uniform(subkeys[1], (clusters, 1), jnp.float32, 0.8, 1.5)
    jitter = jax.random.uniform(subkeys[2], (clusters, 1), jnp.float32, 0.4, 0.8)
    centre_raw = jax.random.normal(subkeys[3], (clusters, D), jnp.float32)
    noise_raw = jax.random.normal(subkeys[4], (NCURVES, D), jnp.float32)
    centres = centre_raw * spread
    picked = jnp.take(centres, member, axis=0)
    noise_scale = jnp.take(jitter, member, axis=0)
    mixed = picked + noise_scale * noise_raw
    return jnp.clip(mixed, -6.0, 6.0).astype(jnp.bfloat16)


def draw_slot_curve(key, part):
    groups = NCURVES // GROUP
    subkeys = jax.random.split(jax.random.fold_in(key, 11), groups)
    orders = jax.vmap(partial(jax.random.permutation, x=GROUP))(subkeys)
    shifted = orders + (jnp.arange(groups, dtype=jnp.int32) * GROUP)[:, None]
    return shifted.reshape(NCURVES).astype(jnp.int32)


def draw_epoch_kernel(key, part):
    subkey = jax.random.fold_in(key, 23)
    factor = jax.random.normal(subkey, (E, E), jnp.float32)
    factor = factor / math.sqrt(E)
    product = jnp.dot(factor, factor.T, precision=lax.Precision.HIGHEST)
    return (jnp.eye(E, dtype=jnp.float32) + 0.5 * product).astype(jnp.float32)


def plant(array, own_key, smallest, top_value):
    index_at = [jax.random.randint(jax.random.fold_in(own_key, axis), (), 0, length) for axis, length in enumerate(array.shape)]
    widest = array.shape.index(max(array.shape))
    neighbour = index_at[:widest] + [(index_at[widest] + 1) % array.shape[widest]] + index_at[widest + 1:]
    return array.at[tuple(index_at)].set(smallest).at[tuple(neighbour)].set(top_value)


def block_levels(own_key, shape, cuts, smallest, high):
    def one(dim, shards_of):
        steps = jax.random.uniform(jax.random.fold_in(jax.random.fold_in(own_key, 6), dim), (shards_of,), jnp.float32, smallest / len(cuts), high / len(cuts))
        return jnp.repeat(jnp.exp(steps), shape[dim] // shards_of).reshape((-1,) + (1,) * (len(shape) - dim - 1))

    level = one(*cuts[0])
    for cut in cuts[1:]:
        level = level * one(*cut)
    return level


def scatter_about(own_key, shape, scale, most, shards=(), held_as=jnp.bfloat16):
    array = scale * jax.random.normal(own_key, shape, jnp.float32)
    if shards:
        array = array * block_levels(own_key, shape, shards, -0.22, 0.18)
    return jnp.clip(array, -most, most).astype(held_as)


def setup_inputs(seed: int = 0) -> dict:
    splits = jax.random.split(jax.random.key(seed), 7)
    curve_embed = draw_curve_embed(jax.random.fold_in(splits[6], 71), 0)
    solution = scatter_about(splits[1], (NCURVES, E), (NCURVES // 16) ** -0.5, 0.5, ((0, 32),), jnp.float32)
    targets = scatter_about(splits[2], (NCURVES, E), 1.0, 6.0, ((0, 32),))
    lengths = plant(jax.random.randint(splits[3], (NCURVES,), 1, E + 1), jax.random.fold_in(splits[3], 1), 1, E).astype(jnp.int32)
    slot_curve = draw_slot_curve(jax.random.fold_in(splits[6], 71), 0)
    epoch_kernel = draw_epoch_kernel(jax.random.fold_in(splits[6], 71), 0)
    return {"curve_embed": curve_embed, "solution": solution, "targets": targets, "lengths": lengths, "slot_curve": slot_curve, "epoch_kernel": epoch_kernel}


def kernel_rows(left_embed, right_embed):
    left_wide = left_embed.astype(jnp.float32)
    right_wide = right_embed.astype(jnp.float32)
    products = jnp.dot(left_embed, right_embed.T, preferred_element_type=jnp.float32)
    distance = jnp.sum(left_wide * left_wide, axis=1)[:, None] + jnp.sum(right_wide * right_wide, axis=1)[None, :] - 2.0 * products
    return jnp.exp(-distance / D)


def reference(curve_embed, solution, targets, lengths, slot_curve, epoch_kernel):
    fitted = jnp.dot(solution, epoch_kernel, precision=lax.Precision.HIGHEST, preferred_element_type=jnp.float32).astype(jnp.bfloat16)
    blocks = NCURVES // GROUP
    embed_blocks = curve_embed.reshape(blocks, GROUP, D)

    def fit_block(row_embed):
        kernel = kernel_rows(row_embed, curve_embed).astype(jnp.bfloat16)
        return jnp.dot(kernel, fitted, preferred_element_type=jnp.float32)

    fitted_sum = lax.map(fit_block, embed_blocks).reshape(NCURVES, E)
    epochs = jnp.arange(E, dtype=jnp.int32)
    observed = epochs[None, :] < lengths[:, None]
    adjoint = jnp.where(observed, targets.astype(jnp.float32) - fitted_sum, jnp.float32(0.0)).astype(jnp.bfloat16)
    adjoint_blocks = adjoint.reshape(blocks, GROUP, E)
    embed_wide = curve_embed.astype(jnp.float32)

    def grad_block(col_sum, inputs):
        row_embed, adjoint_rows = inputs
        kernel = kernel_rows(row_embed, curve_embed)
        link = jnp.dot(adjoint_rows, fitted.T, preferred_element_type=jnp.float32)
        weight = (link * kernel).astype(jnp.bfloat16)
        row_wide = row_embed.astype(jnp.float32)
        across = jnp.dot(weight, curve_embed, preferred_element_type=jnp.float32) - row_wide * jnp.sum(weight, axis=1, dtype=jnp.float32)[:, None]
        down = jnp.dot(weight.T, row_embed, preferred_element_type=jnp.float32) - embed_wide * jnp.sum(weight, axis=0, dtype=jnp.float32)[:, None]
        return col_sum + down, across

    start_sum = jnp.zeros((NCURVES, D), jnp.float32)
    col_sum, row_parts = lax.scan(grad_block, start_sum, (embed_blocks, adjoint_blocks))
    factor = 2.0 / D
    slot_rows = row_parts.reshape(NCURVES, D) * factor
    row_grad = jnp.zeros((NCURVES, D), jnp.float32).at[slot_curve].set(slot_rows)
    col_grad = col_sum * factor
    return row_grad, col_grad
```

```python
import functools
import math

import jax
import jax.numpy as jnp
from jax import lax
from jax.experimental import pallas as pl
from jax.experimental.pallas import tpu as pltpu
from jax.sharding import PartitionSpec as P

GATHER_LIMIT = 4 << 20
BF16, F32 = jnp.bfloat16, jnp.float32
VMEM = pl.BlockSpec(memory_space=pltpu.VMEM)
SMEM = pl.BlockSpec(memory_space=pltpu.SMEM)
PARAMS = pltpu.CompilerParams(vmem_limit_bytes=24 << 20)


def nt_dot(left, right):
    return lax.dot_general(left, right, (((1,), (1,)), ((), ())), preferred_element_type=F32)


def nn_dot(left, right):
    return jnp.dot(left, right, preferred_element_type=F32)


def extended(embed):
    rows, width = embed.shape
    wide = embed.astype(F32)
    square = wide * wide
    high = square.astype(BF16)
    low = (square - high.astype(F32)).astype(BF16)
    ones = jnp.ones((2 * width, width), BF16)
    half = -0.5 * nn_dot(jnp.concatenate([high, low], axis=1), ones)
    first = half.astype(BF16).astype(F32)
    second = (half - first).astype(BF16).astype(F32)
    third = half - first - second
    lane = lax.broadcasted_iota(jnp.int32, (rows, width), 1)

    def lanes(at, one_at):
        tail = jnp.where((lane >= one_at) & (lane < one_at + 3), 1.0, 0.0)
        for offset, term in enumerate((first, second, third)):
            tail = jnp.where(lane == at + offset, term, tail)
        return jnp.concatenate([embed, tail.astype(BF16)], axis=1)

    return lanes


def head_kernel(width, embed_ref, solution_ref, targets_ref, lengths_ref, epoch_ref, out_ref):
    rows, epochs = solution_ref.shape
    fitted = jnp.dot(
        solution_ref[...], epoch_ref[...], precision=lax.Precision.HIGHEST, preferred_element_type=F32
    )
    row = lax.broadcasted_iota(jnp.int32, (rows, rows), 0)
    column = lax.broadcasted_iota(jnp.int32, (rows, rows), 1)
    lengths = jnp.sum(
        jnp.where(row == column, lengths_ref[...], 0).astype(F32), axis=1, keepdims=True
    )
    epoch = lax.broadcasted_iota(jnp.int32, (rows, epochs), 1).astype(F32)
    targets = jnp.where(epoch < lengths, targets_ref[...].astype(F32), jnp.inf)
    out_ref[:, :width] = embed_ref[...]
    out_ref[:, width : width + epochs] = fitted.astype(BF16)
    out_ref[:, width + epochs :] = targets.astype(BF16)


def fit_chunks(left, right_ref, fields_ref, scale, width, chunk):
    total = None
    for at in range(0, fields_ref.shape[0], chunk):
        kernel = jnp.exp2(nt_dot(left, right_ref[at : at + chunk, :]) * scale).astype(BF16)
        part = nn_dot(kernel, fields_ref[at : at + chunk, width:])
        total = part if total is None else total + part
    return total


def block_of(ref, block, rows, mask):
    return pl.ds(pl.multiple_of((lax.axis_index("col") ^ mask) * block, block), rows)


def near_kernel(scale, chunk, near_ref, left_ref, right_ref, fit_ref):
    width = left_ref.shape[1] // 2
    block = near_ref.shape[0] // lax.axis_size("col")
    for part in range(left_ref.shape[0] // block):
        embed = near_ref[block_of(near_ref, block, block, 2 * part), :width]
        left_ref[part * block : (part + 1) * block, :] = extended(embed)(3, 0)
    for at in range(0, near_ref.shape[0], chunk):
        right_ref[at : at + chunk, :] = extended(near_ref[at : at + chunk, :width])(0, 3)
    fit_ref[...] = fit_chunks(left_ref[...], right_ref, near_ref, scale, width, chunk)


def far_kernel(scale, factor, chunk, parts, own, *refs):
    near_ref, far_ref, left_ref, right_near_ref, fit_ref = refs[:5]
    targets_refs, ids_refs = refs[5 : 5 + parts], refs[5 + parts : 5 + 2 * parts]
    col_far_ref, col_near_ref, row_ref, right_far_ref, adjoint_ref = refs[5 + 2 * parts :]
    width = left_ref.shape[1] // 2
    block = near_ref.shape[0] // lax.axis_size("col")
    for at in range(0, far_ref.shape[0], chunk):
        right_far_ref[at : at + chunk, :] = extended(far_ref[at : at + chunk, :width])(0, 3)
    left = left_ref[...]
    fit = fit_ref[...] + fit_chunks(left, right_far_ref, far_ref, scale, width, chunk)
    for part in range(parts):
        rows = slice(part * block, (part + 1) * block)
        targets = targets_refs[part][...].astype(F32)
        adjoint = jnp.where(targets == jnp.inf, 0.0, targets - fit[rows])
        adjoint_ref[rows, :] = adjoint.astype(BF16)
    adjoint = adjoint_ref[...]

    def with_ones(embed):
        return jnp.concatenate([embed, jnp.ones_like(embed)], axis=1)

    def weighted(fields, adjoint, right, left):
        return (nt_dot(fields, adjoint) * jnp.exp2(nt_dot(right, left) * scale)).astype(BF16)

    def gradient(summed, embed):
        return factor * (summed[:, :width] - embed.astype(F32) * summed[:, width:])

    row_sources = with_ones(left[:, :width])
    for fields_ref, right_ref, out_ref in (
        (far_ref, right_far_ref, col_far_ref),
        (near_ref, right_near_ref, col_near_ref),
    ):
        picks = [block_of(fields_ref, block, own, mask) for mask in (0, 1)]
        fields = jnp.concatenate([fields_ref[pick, width:] for pick in picks], axis=0)
        right = jnp.concatenate([right_ref[pick, :] for pick in picks], axis=0)
        summed = nn_dot(weighted(fields, adjoint, right, left), row_sources)
        out_ref[...] = gradient(summed, right[:, :width])

    starts = range(0, parts * block, block)
    slots_left = jnp.concatenate([left_ref[at : at + own, :] for at in starts], axis=0)
    slots_adjoint = jnp.concatenate([adjoint_ref[at : at + own, :] for at in starts], axis=0)
    summed = None
    for fields_ref, right_ref in ((near_ref, right_near_ref), (far_ref, right_far_ref)):
        for at in range(0, fields_ref.shape[0], chunk):
            run = slice(at, at + chunk)
            weight = weighted(slots_adjoint, fields_ref[run, width:], slots_left, right_ref[run, :])
            part = nn_dot(weight, with_ones(fields_ref[run, :width]))
            summed = part if summed is None else summed + part
    slot_rows = gradient(summed, slots_left[:, :width])
    ids = jnp.concatenate([jnp.broadcast_to(ref[...], (own, own)) for ref in ids_refs], axis=1)
    wanted = lax.broadcasted_iota(jnp.int32, ids.shape, 0)
    first = lax.axis_index("row") * lax.axis_size("col")
    for mask in (0, 1):
        base = (first + (lax.axis_index("col") ^ mask)) * own
        chosen = (ids == wanted + base).astype(F32)
        row_ref[mask * own : (mask + 1) * own, :] = jnp.dot(
            chosen, slot_rows, precision=lax.Precision.HIGHEST, preferred_element_type=F32
        )


def swap(array, axis, mask):
    pairs = [(index, index ^ mask) for index in range(lax.axis_size(axis))]
    return lax.ppermute(array, axis, pairs)


def joined(array, axis, mask):
    return jnp.concatenate([array, swap(array, axis, mask)], axis=0)


def gathered_plan(curve_embed, solution, targets, lengths, slot_curve, epoch_kernel):
    own, width = curve_embed.shape
    epochs = solution.shape[1]
    rows_axis, cols_axis = lax.axis_size("row"), lax.axis_size("col")
    scale = 2.0 * math.log2(math.e) / width
    factor = 2.0 / width
    shape = jax.ShapeDtypeStruct

    packed = pl.pallas_call(
        functools.partial(head_kernel, width),
        out_shape=shape((own, width + 2 * epochs), BF16),
        in_specs=[VMEM] * 5,
        out_specs=VMEM,
        compiler_params=PARAMS,
    )(curve_embed, solution, targets, lengths.reshape(1, own), epoch_kernel)
    columns, observed = packed[:, : width + epochs], packed[:, width + epochs :]
    step = 2
    if step < rows_axis:
        other = swap(packed, "row", step)
        columns = jnp.concatenate([columns, other[:, : width + epochs]], axis=0)
        observed = jnp.concatenate([observed, other[:, width + epochs :]], axis=0)
        step *= 2
    while step < rows_axis:
        columns, observed = joined(columns, "row", step), joined(observed, "row", step)
        step *= 2
    near = lax.all_gather(columns, "col", axis=0, tiled=True)
    far = swap(near, "row", 1)
    observed, ids = [observed], [slot_curve.reshape(1, own)]
    step = 2
    while step < cols_axis:
        observed += [swap(array, "col", step) for array in observed]
        ids += [swap(array, "col", step) for array in ids]
        step *= 2
    parts, block, half = len(observed), observed[0].shape[0], near.shape[0]
    held, chunk = parts * block, block
    left, right, fit = pl.pallas_call(
        functools.partial(near_kernel, scale, chunk),
        out_shape=(shape((held, 2 * width), BF16), shape((half, 2 * width), BF16), shape((held, epochs), F32)),
        in_specs=[VMEM],
        out_specs=[VMEM] * 3,
        compiler_params=PARAMS,
        cost_estimate=pl.CostEstimate(
            flops=2 * held * half * (2 * width + epochs), bytes_accessed=2 << 20, transcendentals=held * half
        ),
    )(near)
    col_far, col_near, row_part = pl.pallas_call(
        functools.partial(far_kernel, scale, factor, chunk, parts, own),
        out_shape=(shape((2 * own, width), F32),) * 3,
        in_specs=[VMEM] * (5 + 2 * parts),
        out_specs=[VMEM] * 3,
        scratch_shapes=[pltpu.VMEM((half, 2 * width), BF16), pltpu.VMEM((held, epochs), BF16)],
        compiler_params=PARAMS,
    )(near, far, left, right, fit, *observed, *ids)
    col_part = col_near + swap(col_far, "row", 1)
    other = swap(jnp.concatenate([col_part[own:], row_part[own:]], axis=0), "col", 1)
    return row_part[:own] + other[own:], col_part[:own] + other[:own]


def kernel_block(row_embed, row_square, piece_embed):
    piece_wide = piece_embed.astype(jnp.float32)
    products = lax.dot_general(
        row_embed, piece_embed, (((1,), (1,)), ((), ())), preferred_element_type=jnp.float32
    )
    distance = (
        row_square[:, None] + jnp.sum(piece_wide * piece_wide, axis=1)[None, :] - 2.0 * products
    )
    return jnp.exp(-distance / row_embed.shape[1])


def block_width():
    return 256


def make_fit(row_embed, row_square):

    def fit_fold(summed, pieces, offset):
        piece_embed, piece_fitted = pieces
        extent = piece_embed.shape[0]
        width_blk = block_width()

        def fit_advance(position, running):
            embed_part = lax.dynamic_slice_in_dim(piece_embed, position * width_blk, width_blk, 0)
            fitted_part = lax.dynamic_slice_in_dim(piece_fitted, position * width_blk, width_blk, 0)
            kernel = kernel_block(row_embed, row_square, embed_part).astype(jnp.bfloat16)
            return running + jnp.dot(kernel, fitted_part, preferred_element_type=jnp.float32)

        return lax.fori_loop(0, extent // width_blk, fit_advance, summed)

    return fit_fold


def make_grad(row_embed, row_square, row_wide, adjoint):

    def grad_fold(carry, pieces, offset):
        piece_embed, piece_fitted = pieces
        extent = piece_embed.shape[0]
        width_blk = block_width()

        def grad_advance(position, running):
            row_part, col_part = running
            embed_part = lax.dynamic_slice_in_dim(piece_embed, position * width_blk, width_blk, 0)
            fitted_part = lax.dynamic_slice_in_dim(piece_fitted, position * width_blk, width_blk, 0)
            kernel = kernel_block(row_embed, row_square, embed_part)
            link = lax.dot_general(
                adjoint, fitted_part, (((1,), (1,)), ((), ())), preferred_element_type=jnp.float32
            )
            weight = (link * kernel).astype(jnp.bfloat16)
            across = (
                jnp.dot(weight, embed_part, preferred_element_type=jnp.float32)
                - row_wide * jnp.sum(weight, axis=1, dtype=jnp.float32)[:, None]
            )
            down = lax.dot_general(
                weight, row_embed, (((0,), (0,)), ((), ())), preferred_element_type=jnp.float32
            )
            down = (
                down
                - embed_part.astype(jnp.float32)
                * jnp.sum(weight, axis=0, dtype=jnp.float32)[:, None]
            )
            first_row = offset + position * width_blk
            col_part = lax.dynamic_update_slice_in_dim(col_part, down, first_row, 0)
            return (row_part + across, col_part)

        return lax.fori_loop(0, extent // width_blk, grad_advance, carry)

    return grad_fold


def tiled_plan(curve_embed, solution, targets, lengths, slot_curve, epoch_kernel):
    own_rows = curve_embed.shape[0]
    width = curve_embed.shape[1]
    epochs_count = solution.shape[1]
    group_size = own_rows * lax.axis_size("col")
    column_size = own_rows * lax.axis_size("row")
    fitted_own = jnp.dot(
        solution, epoch_kernel, precision=lax.Precision.HIGHEST, preferred_element_type=jnp.float32
    ).astype(jnp.bfloat16)
    row_embed, row_curve = (
        lax.all_gather(curve_embed, "col", axis=0, tiled=True),
        lax.all_gather(slot_curve, "col", axis=0, tiled=True),
    )
    row_wide = row_embed.astype(jnp.float32)
    row_square = jnp.sum(row_wide * row_wide, axis=1)
    fit_fold = make_fit(row_embed, row_square)
    start_fit = jnp.zeros((group_size, epochs_count), jnp.float32)
    col_embed, col_fitted = (
        lax.all_gather(curve_embed, "row", axis=0, tiled=True),
        lax.all_gather(fitted_own, "row", axis=0, tiled=True),
    )
    fitted_sum = fit_fold(start_fit, (col_embed, col_fitted), 0)
    epochs = jnp.arange(epochs_count, dtype=jnp.int32)
    fitted_mine = lax.psum_scatter(fitted_sum, "col", scatter_dimension=0, tiled=True)
    observed = epochs[None, :] < lengths[:, None]
    adjoint_own = jnp.where(observed, targets.astype(jnp.float32) - fitted_mine, 0.0).astype(
        jnp.bfloat16
    )
    adjoint = lax.all_gather(adjoint_own, "col", axis=0, tiled=True)
    grad_fold = make_grad(row_embed, row_square, row_wide, adjoint)
    start_grad = (
        jnp.zeros((group_size, width), jnp.float32),
        jnp.zeros((column_size, width), jnp.float32),
    )
    row_sum, col_sum = grad_fold(start_grad, (col_embed, col_fitted), 0)
    group_base = lax.axis_index("row") * group_size
    local_curve = (row_curve - group_base).astype(jnp.int32)
    inverse = (
        jnp.zeros((group_size,), jnp.int32)
        .at[local_curve]
        .set(jnp.arange(group_size, dtype=jnp.int32))
    )
    reordered = jnp.take(row_sum, inverse, axis=0)
    factor = 2.0 / width
    row_grad = lax.psum_scatter(reordered, "col", scatter_dimension=0, tiled=True) * factor
    col_grad = lax.psum_scatter(col_sum, "row", scatter_dimension=0, tiled=True) * factor
    return (row_grad, col_grad)


def power_of_two(number):
    return number >= 2 and number & (number - 1) == 0


def per_device(curve_embed, solution, *rest):
    own, width = curve_embed.shape
    rows_axis, cols_axis = lax.axis_size("row"), lax.axis_size("col")
    gathered = own * rows_axis * cols_axis * (width + solution.shape[1]) * 2
    if gathered <= GATHER_LIMIT and power_of_two(rows_axis) and power_of_two(cols_axis):
        return gathered_plan(curve_embed, solution, *rest)
    return tiled_plan(curve_embed, solution, *rest)


def solution(mesh):
    in_specs = (
        P(("row", "col"), None),
        P(("row", "col"), None),
        P(("row", "col"), None),
        P(("row", "col")),
        P(("row", "col")),
        P(),
    )
    out_specs = (P(("row", "col"), None), P(("row", "col"), None))
    return jax.shard_map(
        per_device, mesh=mesh, in_specs=in_specs, out_specs=out_specs, check_vma=False
    )
```

```python
import functools
import math

import jax
import jax.numpy as jnp
from jax import lax
from jax.experimental import pallas as pl
from jax.experimental.pallas import tpu as pltpu
from jax.sharding import PartitionSpec as P

GATHER_LIMIT = 4 << 20
BF16, F32 = jnp.bfloat16, jnp.float32
VMEM = pl.BlockSpec(memory_space=pltpu.VMEM)
SMEM = pl.BlockSpec(memory_space=pltpu.SMEM)
PARAMS = pltpu.CompilerParams(vmem_limit_bytes=24 << 20)


def nt_dot(left, right):
    return lax.dot_general(left, right, (((1,), (1,)), ((), ())), preferred_element_type=F32)


def nn_dot(left, right):
    return jnp.dot(left, right, preferred_element_type=F32)


def extended(embed):
    rows, width = embed.shape
    wide = embed.astype(F32)
    square = wide * wide
    high = square.astype(BF16)
    low = (square - high.astype(F32)).astype(BF16)
    ones = jnp.ones((2 * width, width), BF16)
    half = -0.5 * nn_dot(jnp.concatenate([high, low], axis=1), ones)
    first = half.astype(BF16).astype(F32)
    second = (half - first).astype(BF16).astype(F32)
    third = half - first - second
    lane = lax.broadcasted_iota(jnp.int32, (rows, width), 1)

    def lanes(at, one_at):
        tail = jnp.where((lane >= one_at) & (lane < one_at + 3), 1.0, 0.0)
        for offset, term in enumerate((first, second, third)):
            tail = jnp.where(lane == at + offset, term, tail)
        return jnp.concatenate([embed, tail.astype(BF16)], axis=1)

    return lanes


def head_kernel(width, *refs):
    out_ref, held, semaphores = refs[5], refs[6:11], refs[11]
    copies = [
        pltpu.make_async_copy(source, target, semaphores.at[index])
        for index, (source, target) in enumerate(zip(refs[:5], held))
    ]
    for copy in copies:
        copy.start()
    for copy in copies:
        copy.wait()
    embed_ref, solution_ref, targets_ref, lengths_ref, epoch_ref = held
    rows, epochs = solution_ref.shape
    fitted = jnp.dot(
        solution_ref[...], epoch_ref[...], precision=lax.Precision.HIGHEST, preferred_element_type=F32
    )
    row = lax.broadcasted_iota(jnp.int32, (rows, rows), 0)
    column = lax.broadcasted_iota(jnp.int32, (rows, rows), 1)
    lengths = jnp.sum(
        jnp.where(row == column, lengths_ref[...], 0).astype(F32), axis=1, keepdims=True
    )
    epoch = lax.broadcasted_iota(jnp.int32, (rows, epochs), 1).astype(F32)
    targets = jnp.where(epoch < lengths, targets_ref[...].astype(F32), jnp.inf)
    out_ref[:, :width] = embed_ref[...]
    out_ref[:, width : width + epochs] = fitted.astype(BF16)
    out_ref[:, width + epochs :] = targets.astype(BF16)


def fit_chunks(left, right_ref, fields_ref, scale, width, chunk):
    total = None
    for at in range(0, fields_ref.shape[0], chunk):
        kernel = jnp.exp2(nt_dot(left, right_ref[at : at + chunk, :]) * scale).astype(BF16)
        part = nn_dot(kernel, fields_ref[at : at + chunk, width:])
        total = part if total is None else total + part
    return total


def block_of(ref, block, rows, mask):
    return pl.ds(pl.multiple_of((lax.axis_index("col") ^ mask) * block, block), rows)


def near_kernel(scale, chunk, near_ref, left_ref, right_ref, fit_ref):
    width = left_ref.shape[1] // 2
    block = near_ref.shape[0] // lax.axis_size("col")
    for part in range(left_ref.shape[0] // block):
        embed = near_ref[block_of(near_ref, block, block, 2 * part), :width]
        left_ref[part * block : (part + 1) * block, :] = extended(embed)(3, 0)
    for at in range(0, near_ref.shape[0], chunk):
        right_ref[at : at + chunk, :] = extended(near_ref[at : at + chunk, :width])(0, 3)
    fit_ref[...] = fit_chunks(left_ref[...], right_ref, near_ref, scale, width, chunk)


def with_ones(embed):
    return jnp.concatenate([embed, jnp.ones_like(embed)], axis=1)


def weighted(scale, fields, adjoint, right, left):
    return (nt_dot(fields, adjoint) * jnp.exp2(nt_dot(right, left) * scale)).astype(BF16)


def gradient(factor, summed, embed):
    width = embed.shape[1]
    return factor * (summed[:, :width] - embed.astype(F32) * summed[:, width:])


def column_part(scale, factor, own, adjoint, left, fields_ref, right_ref):
    width = left.shape[1] // 2
    block = fields_ref.shape[0] // lax.axis_size("col")
    picks = [block_of(fields_ref, block, own, mask) for mask in (0, 1)]
    fields = jnp.concatenate([fields_ref[pick, width:] for pick in picks], axis=0)
    right = jnp.concatenate([right_ref[pick, :] for pick in picks], axis=0)
    weight = weighted(scale, fields, adjoint, right, left)
    return gradient(factor, nn_dot(weight, with_ones(left[:, :width])), right[:, :width])


def far_kernel(scale, factor, chunk, parts, own, run, *refs):
    far_ref, left_ref, fit_ref, targets_ref, right_ref, adjoint_ref, col_ref = refs
    width = left_ref.shape[1] // 2
    held = left_ref.shape[0]
    for at in range(0, far_ref.shape[0], chunk):
        right_ref[at : at + chunk, :] = extended(far_ref[at : at + chunk, :width])(0, 3)
    left = left_ref[...]
    fit = fit_ref[...] + fit_chunks(left, right_ref, far_ref, scale, width, chunk)
    for at in range(0, held, run):
        part, piece = divmod(at, held // parts)
        first = piece * parts + part * run
        targets = targets_ref[first : first + run, :].astype(F32)
        adjoint = jnp.where(targets == jnp.inf, 0.0, targets - fit[at : at + run])
        adjoint_ref[at : at + run, :] = adjoint.astype(BF16)
    col_ref[...] = column_part(scale, factor, own, adjoint_ref[...], left, far_ref, right_ref)


def last_kernel(scale, factor, chunk, parts, own, *refs):
    near_ref, far_ref, left_ref, right_near_ref, right_far_ref, adjoint_ref = refs[:6]
    ids_refs, (col_ref, row_ref) = refs[6 : 6 + parts], refs[6 + parts :]
    width = left_ref.shape[1] // 2
    block = left_ref.shape[0] // parts
    col_ref[...] = column_part(
        scale, factor, own, adjoint_ref[...], left_ref[...], near_ref, right_near_ref
    )
    starts = range(0, parts * block, block)
    slots_left = jnp.concatenate([left_ref[at : at + own, :] for at in starts], axis=0)
    slots_adjoint = jnp.concatenate([adjoint_ref[at : at + own, :] for at in starts], axis=0)
    summed = None
    for fields_ref, right_ref in ((near_ref, right_near_ref), (far_ref, right_far_ref)):
        for at in range(0, fields_ref.shape[0], chunk):
            span = slice(at, at + chunk)
            weight = weighted(
                scale, slots_adjoint, fields_ref[span, width:], slots_left, right_ref[span, :]
            )
            part = nn_dot(weight, with_ones(fields_ref[span, :width]))
            summed = part if summed is None else summed + part
    slot_rows = gradient(factor, summed, slots_left[:, :width])
    ids = jnp.concatenate([jnp.broadcast_to(ref[...], (own, own)) for ref in ids_refs], axis=1)
    wanted = lax.broadcasted_iota(jnp.int32, ids.shape, 0)
    first = lax.axis_index("row") * lax.axis_size("col")
    for mask in (0, 1):
        base = (first + (lax.axis_index("col") ^ mask)) * own
        chosen = (ids == wanted + base).astype(F32)
        row_ref[mask * own : (mask + 1) * own, :] = jnp.dot(
            chosen, slot_rows, precision=lax.Precision.HIGHEST, preferred_element_type=F32
        )


def swap(array, axis, mask):
    pairs = [(index, index ^ mask) for index in range(lax.axis_size(axis))]
    return lax.ppermute(array, axis, pairs)


def joined(array, axis, mask):
    return jnp.concatenate([array, swap(array, axis, mask)], axis=0)


def gathered_plan(curve_embed, solution, targets, lengths, slot_curve, epoch_kernel):
    own, width = curve_embed.shape
    epochs = solution.shape[1]
    rows_axis, cols_axis = lax.axis_size("row"), lax.axis_size("col")
    scale = 2.0 * math.log2(math.e) / width
    factor = 2.0 / width
    shape = jax.ShapeDtypeStruct

    arrays = (curve_embed, solution, targets, lengths.reshape(1, own), epoch_kernel)
    packed = pl.pallas_call(
        functools.partial(head_kernel, width),
        out_shape=shape((own, width + 2 * epochs), BF16),
        in_specs=[pl.BlockSpec(memory_space=pltpu.HBM)] * 5,
        out_specs=VMEM,
        scratch_shapes=[
            *(pltpu.VMEM(array.shape, array.dtype) for array in arrays),
            pltpu.SemaphoreType.DMA((5,)),
        ],
    )(*arrays)
    columns, observed = packed[:, : width + epochs], packed[:, width + epochs :]
    ids = [slot_curve.reshape(1, own)]
    step = 2
    if step < rows_axis:
        other = swap(packed, "row", step)
        columns = jnp.concatenate([columns, other[:, : width + epochs]], axis=0)
        observed = jnp.concatenate([observed, other[:, width + epochs :]], axis=0)
        step *= 2
    run = observed.shape[0]
    turn = 2
    while turn < cols_axis:
        observed = joined(observed, "col", turn)
        ids += [swap(array, "col", turn) for array in ids]
        turn *= 2
    observed, ids = lax.optimization_barrier((observed, ids))
    while step < rows_axis:
        columns, observed = joined(columns, "row", step), joined(observed, "row", step)
        step *= 2
    near = lax.all_gather(columns, "col", axis=0, tiled=True)
    near, observed = lax.optimization_barrier((near, observed))
    far = swap(near, "row", 1)
    parts, held, half = len(ids), observed.shape[0], near.shape[0]
    chunk = columns.shape[0]
    left, right_near, fit = pl.pallas_call(
        functools.partial(near_kernel, scale, chunk),
        out_shape=(
            shape((held, 2 * width), BF16),
            shape((half, 2 * width), BF16),
            shape((held, epochs), F32),
        ),
        in_specs=[VMEM],
        out_specs=[VMEM] * 3,
        compiler_params=PARAMS,
        cost_estimate=pl.CostEstimate(
            flops=2 * held * half * (2 * width + epochs),
            bytes_accessed=2 << 20,
            transcendentals=held * half,
        ),
    )(near)
    right_far, adjoint, col_far = pl.pallas_call(
        functools.partial(far_kernel, scale, factor, chunk, parts, own, run),
        out_shape=(
            shape((half, 2 * width), BF16),
            shape((held, epochs), BF16),
            shape((2 * own, width), F32),
        ),
        in_specs=[VMEM] * 4,
        out_specs=[VMEM] * 3,
        compiler_params=PARAMS,
    )(far, left, fit, observed)
    col_other = swap(col_far, "row", 1)
    col_near, row_part = pl.pallas_call(
        functools.partial(last_kernel, scale, factor, chunk, parts, own),
        out_shape=(shape((2 * own, width), F32),) * 2,
        in_specs=[VMEM] * (6 + parts),
        out_specs=[VMEM] * 2,
        compiler_params=PARAMS,
        cost_estimate=pl.CostEstimate(
            flops=2 * held * half * (2 * width + epochs),
            bytes_accessed=2 << 20,
            transcendentals=held * half,
        ),
    )(near, far, left, right_near, right_far, adjoint, *ids)
    col_part = col_near + col_other
    other = swap(jnp.concatenate([col_part[own:], row_part[own:]], axis=0), "col", 1)
    return row_part[:own] + other[own:], col_part[:own] + other[:own]


def kernel_block(row_embed, row_square, piece_embed):
    piece_wide = piece_embed.astype(jnp.float32)
    products = lax.dot_general(
        row_embed, piece_embed, (((1,), (1,)), ((), ())), preferred_element_type=jnp.float32
    )
    distance = (
        row_square[:, None] + jnp.sum(piece_wide * piece_wide, axis=1)[None, :] - 2.0 * products
    )
    return jnp.exp(-distance / row_embed.shape[1])


def block_width():
    return 256


def make_fit(row_embed, row_square):

    def fit_fold(summed, pieces, offset):
        piece_embed, piece_fitted = pieces
        extent = piece_embed.shape[0]
        width_blk = block_width()

        def fit_advance(position, running):
            embed_part = lax.dynamic_slice_in_dim(piece_embed, position * width_blk, width_blk, 0)
            fitted_part = lax.dynamic_slice_in_dim(piece_fitted, position * width_blk, width_blk, 0)
            kernel = kernel_block(row_embed, row_square, embed_part).astype(jnp.bfloat16)
            return running + jnp.dot(kernel, fitted_part, preferred_element_type=jnp.float32)

        return lax.fori_loop(0, extent // width_blk, fit_advance, summed)

    return fit_fold


def make_grad(row_embed, row_square, row_wide, adjoint):

    def grad_fold(carry, pieces, offset):
        piece_embed, piece_fitted = pieces
        extent = piece_embed.shape[0]
        width_blk = block_width()

        def grad_advance(position, running):
            row_part, col_part = running
            embed_part = lax.dynamic_slice_in_dim(piece_embed, position * width_blk, width_blk, 0)
            fitted_part = lax.dynamic_slice_in_dim(piece_fitted, position * width_blk, width_blk, 0)
            kernel = kernel_block(row_embed, row_square, embed_part)
            link = lax.dot_general(
                adjoint, fitted_part, (((1,), (1,)), ((), ())), preferred_element_type=jnp.float32
            )
            weight = (link * kernel).astype(jnp.bfloat16)
            across = (
                jnp.dot(weight, embed_part, preferred_element_type=jnp.float32)
                - row_wide * jnp.sum(weight, axis=1, dtype=jnp.float32)[:, None]
            )
            down = lax.dot_general(
                weight, row_embed, (((0,), (0,)), ((), ())), preferred_element_type=jnp.float32
            )
            down = (
                down
                - embed_part.astype(jnp.float32)
                * jnp.sum(weight, axis=0, dtype=jnp.float32)[:, None]
            )
            first_row = offset + position * width_blk
            col_part = lax.dynamic_update_slice_in_dim(col_part, down, first_row, 0)
            return (row_part + across, col_part)

        return lax.fori_loop(0, extent // width_blk, grad_advance, carry)

    return grad_fold


def tiled_plan(curve_embed, solution, targets, lengths, slot_curve, epoch_kernel):
    own_rows = curve_embed.shape[0]
    width = curve_embed.shape[1]
    epochs_count = solution.shape[1]
    group_size = own_rows * lax.axis_size("col")
    column_size = own_rows * lax.axis_size("row")
    fitted_own = jnp.dot(
        solution, epoch_kernel, precision=lax.Precision.HIGHEST, preferred_element_type=jnp.float32
    ).astype(jnp.bfloat16)
    row_embed, row_curve = (
        lax.all_gather(curve_embed, "col", axis=0, tiled=True),
        lax.all_gather(slot_curve, "col", axis=0, tiled=True),
    )
    row_wide = row_embed.astype(jnp.float32)
    row_square = jnp.sum(row_wide * row_wide, axis=1)
    fit_fold = make_fit(row_embed, row_square)
    start_fit = jnp.zeros((group_size, epochs_count), jnp.float32)
    col_embed, col_fitted = (
        lax.all_gather(curve_embed, "row", axis=0, tiled=True),
        lax.all_gather(fitted_own, "row", axis=0, tiled=True),
    )
    fitted_sum = fit_fold(start_fit, (col_embed, col_fitted), 0)
    epochs = jnp.arange(epochs_count, dtype=jnp.int32)
    fitted_mine = lax.psum_scatter(fitted_sum, "col", scatter_dimension=0, tiled=True)
    observed = epochs[None, :] < lengths[:, None]
    adjoint_own = jnp.where(observed, targets.astype(jnp.float32) - fitted_mine, 0.0).astype(
        jnp.bfloat16
    )
    adjoint = lax.all_gather(adjoint_own, "col", axis=0, tiled=True)
    grad_fold = make_grad(row_embed, row_square, row_wide, adjoint)
    start_grad = (
        jnp.zeros((group_size, width), jnp.float32),
        jnp.zeros((column_size, width), jnp.float32),
    )
    row_sum, col_sum = grad_fold(start_grad, (col_embed, col_fitted), 0)
    group_base = lax.axis_index("row") * group_size
    local_curve = (row_curve - group_base).astype(jnp.int32)
    inverse = (
        jnp.zeros((group_size,), jnp.int32)
        .at[local_curve]
        .set(jnp.arange(group_size, dtype=jnp.int32))
    )
    reordered = jnp.take(row_sum, inverse, axis=0)
    factor = 2.0 / width
    row_grad = lax.psum_scatter(reordered, "col", scatter_dimension=0, tiled=True) * factor
    col_grad = lax.psum_scatter(col_sum, "row", scatter_dimension=0, tiled=True) * factor
    return (row_grad, col_grad)


def power_of_two(number):
    return number >= 2 and number & (number - 1) == 0


def per_device(curve_embed, solution, *rest):
    own, width = curve_embed.shape
    rows_axis, cols_axis = lax.axis_size("row"), lax.axis_size("col")
    gathered = own * rows_axis * cols_axis * (width + solution.shape[1]) * 2
    if gathered <= GATHER_LIMIT and power_of_two(rows_axis) and power_of_two(cols_axis):
        return gathered_plan(curve_embed, solution, *rest)
    return tiled_plan(curve_embed, solution, *rest)


def solution(mesh):
    in_specs = (
        P(("row", "col"), None),
        P(("row", "col"), None),
        P(("row", "col"), None),
        P(("row", "col")),
        P(("row", "col")),
        P(),
    )
    out_specs = (P(("row", "col"), None), P(("row", "col"), None))
    return jax.shard_map(
        per_device, mesh=mesh, in_specs=in_specs, out_specs=out_specs, check_vma=False
    )
```

```python
import functools
import math

import jax
import jax.numpy as jnp
from jax import lax
from jax.experimental import pallas as pl
from jax.experimental.pallas import tpu as pltpu
from jax.sharding import PartitionSpec as P

GATHER_LIMIT = 4 << 20
BF16, F32 = jnp.bfloat16, jnp.float32
VMEM = pl.BlockSpec(memory_space=pltpu.VMEM)
SMEM = pl.BlockSpec(memory_space=pltpu.SMEM)
PARAMS = pltpu.CompilerParams(vmem_limit_bytes=24 << 20)


def nt_dot(left, right):
    return lax.dot_general(left, right, (((1,), (1,)), ((), ())), preferred_element_type=F32)


def nn_dot(left, right):
    return jnp.dot(left, right, preferred_element_type=F32)


def extended(embed):
    rows, width = embed.shape
    wide = embed.astype(F32)
    square = wide * wide
    high = square.astype(BF16)
    low = (square - high.astype(F32)).astype(BF16)
    ones = jnp.ones((2 * width, width), BF16)
    half = -0.5 * nn_dot(jnp.concatenate([high, low], axis=1), ones)
    first = half.astype(BF16).astype(F32)
    second = (half - first).astype(BF16).astype(F32)
    third = half - first - second
    lane = lax.broadcasted_iota(jnp.int32, (rows, width), 1)

    def lanes(at, one_at):
        tail = jnp.where((lane >= one_at) & (lane < one_at + 3), 1.0, 0.0)
        for offset, term in enumerate((first, second, third)):
            tail = jnp.where(lane == at + offset, term, tail)
        return jnp.concatenate([embed, tail.astype(BF16)], axis=1)

    return lanes


def head_kernel(width, *refs):
    out_ref, columns_ref, observed_ref = refs[5:8]
    held, semaphores = refs[8:13], refs[13]
    copies = [
        pltpu.make_async_copy(source, target, semaphores.at[index])
        for index, (source, target) in enumerate(zip(refs[:5], held))
    ]
    for copy in copies:
        copy.start()
    for copy in copies:
        copy.wait()
    embed_ref, solution_ref, targets_ref, lengths_ref, epoch_ref = held
    rows, epochs = solution_ref.shape
    fitted = jnp.dot(
        solution_ref[...], epoch_ref[...], precision=lax.Precision.HIGHEST, preferred_element_type=F32
    )
    row = lax.broadcasted_iota(jnp.int32, (rows, rows), 0)
    column = lax.broadcasted_iota(jnp.int32, (rows, rows), 1)
    lengths = jnp.sum(
        jnp.where(row == column, lengths_ref[...], 0).astype(F32), axis=1, keepdims=True
    )
    epoch = lax.broadcasted_iota(jnp.int32, (rows, epochs), 1).astype(F32)
    targets = jnp.where(epoch < lengths, targets_ref[...].astype(F32), jnp.inf)
    columns = jnp.concatenate([embed_ref[...], fitted.astype(BF16)], axis=1)
    columns_ref[...] = columns
    observed_ref[...] = targets.astype(BF16)
    out_ref[:, : width + epochs] = columns
    out_ref[:, width + epochs :] = targets.astype(BF16)


def observed_kernel(first, own_ref, other_ref, out_ref):
    out_ref[: own_ref.shape[0], :] = own_ref[...]
    out_ref[own_ref.shape[0] :, :] = other_ref[:, first:]


def block_of(block, rows, mask):
    return pl.ds(pl.multiple_of((lax.axis_index("col") ^ mask) * block, block), rows)


def with_ones(embed):
    return jnp.concatenate([embed, jnp.ones_like(embed)], axis=1)


def gradient(factor, summed, embed):
    width = embed.shape[1]
    return factor * (summed[:, :width] - embed.astype(F32) * summed[:, width:])


def slot_runs(ref, own, block):
    return jnp.concatenate(
        [ref[at : at + own, :] for at in range(0, ref.shape[0], block)], axis=0
    )


def fit_part(scale, chunk, own, columns_ref, left_ref, right_ref, slots_ref, picks_ref):
    width = left_ref.shape[1] // 2
    left = left_ref[...]
    slots_left = slot_runs(left_ref, own, chunk)
    total = None
    for at in range(0, columns_ref.shape[0], chunk):
        span = slice(at, at + chunk)
        right = extended(columns_ref[span, :width])(0, 3)
        right_ref[span, :] = right
        kernel = jnp.exp2(nt_dot(left, right) * scale).astype(BF16)
        part = nn_dot(kernel, columns_ref[span, width:])
        total = part if total is None else total + part
        slots_ref[:, span] = jnp.exp2(nt_dot(slots_left, right) * scale)
    for mask in (0, 1):
        right = right_ref[block_of(chunk, own, mask), :]
        picks_ref[mask * own : (mask + 1) * own, :] = jnp.exp2(nt_dot(right, left) * scale)
    return total


def near_kernel(scale, chunk, own, near_ref, left_ref, fit_ref, slots_ref, picks_ref, right_ref):
    width = left_ref.shape[1] // 2
    for part in range(left_ref.shape[0] // chunk):
        embed = near_ref[block_of(chunk, chunk, 2 * part), :width]
        left_ref[part * chunk : (part + 1) * chunk, :] = extended(embed)(3, 0)
    fit_ref[...] = fit_part(
        scale, chunk, own, near_ref, left_ref, right_ref, slots_ref, picks_ref
    )


def far_kernel(scale, chunk, own, far_ref, left_ref, near_fit_ref, fit_ref, slots_ref, picks_ref, right_ref):
    fit_ref[...] = near_fit_ref[...] + fit_part(
        scale, chunk, own, far_ref, left_ref, right_ref, slots_ref, picks_ref
    )


def column_part(factor, own, block, adjoint, embed, columns_ref, kernel_ref):
    width = embed.shape[1]
    columns = jnp.concatenate(
        [columns_ref[block_of(block, own, mask), :] for mask in (0, 1)], axis=0
    )
    weight = (nt_dot(columns[:, width:], adjoint) * kernel_ref[...]).astype(BF16)
    return gradient(factor, nn_dot(weight, with_ones(embed)), columns[:, :width])


def adjoint_kernel(factor, own, far_ref, left_ref, fit_ref, kernel_ref, *refs):
    targets_refs, (adjoint_ref, col_ref) = refs[:-2], refs[-2:]
    width = left_ref.shape[1] // 2
    block = targets_refs[0].shape[0]
    for part, targets_ref in enumerate(targets_refs):
        span = slice(part * block, (part + 1) * block)
        targets = targets_ref[...].astype(F32)
        adjoint = jnp.where(targets == jnp.inf, 0.0, targets - fit_ref[span, :])
        adjoint_ref[span, :] = adjoint.astype(BF16)
    embed = left_ref[:, :width]
    col_ref[...] = column_part(factor, own, block, adjoint_ref[...], embed, far_ref, kernel_ref)


def last_kernel(factor, chunk, parts, own, *refs):
    near_ref, far_ref, left_ref, adjoint_ref, near_slots_ref, picks_ref, far_slots_ref = refs[:7]
    ids_refs, (col_ref, row_ref) = refs[7 : 7 + parts], refs[7 + parts :]
    width = left_ref.shape[1] // 2
    embed = left_ref[:, :width]
    col_ref[...] = column_part(factor, own, chunk, adjoint_ref[...], embed, near_ref, picks_ref)
    slots_embed = slot_runs(left_ref, own, chunk)[:, :width]
    slots_adjoint = slot_runs(adjoint_ref, own, chunk)
    summed = None
    for columns_ref, kernel_ref in ((near_ref, near_slots_ref), (far_ref, far_slots_ref)):
        for at in range(0, columns_ref.shape[0], chunk):
            span = slice(at, at + chunk)
            link = nt_dot(slots_adjoint, columns_ref[span, width:])
            weight = (link * kernel_ref[:, span]).astype(BF16)
            part = nn_dot(weight, with_ones(columns_ref[span, :width]))
            summed = part if summed is None else summed + part
    slot_rows = gradient(factor, summed, slots_embed)
    ids = jnp.concatenate([jnp.broadcast_to(ref[...], (own, own)) for ref in ids_refs], axis=1)
    wanted = lax.broadcasted_iota(jnp.int32, ids.shape, 0)
    first = lax.axis_index("row") * lax.axis_size("col")
    for mask in (0, 1):
        base = (first + (lax.axis_index("col") ^ mask)) * own
        chosen = (ids == wanted + base).astype(F32)
        row_ref[mask * own : (mask + 1) * own, :] = jnp.dot(
            chosen, slot_rows, precision=lax.Precision.HIGHEST, preferred_element_type=F32
        )


def swap(array, axis, mask):
    pairs = [(index, index ^ mask) for index in range(lax.axis_size(axis))]
    return lax.ppermute(array, axis, pairs)


def joined(array, axis, mask):
    return jnp.concatenate([array, swap(array, axis, mask)], axis=0)


def gathered_plan(curve_embed, solution, targets, lengths, slot_curve, epoch_kernel):
    own, width = curve_embed.shape
    epochs = solution.shape[1]
    rows_axis, cols_axis = lax.axis_size("row"), lax.axis_size("col")
    scale = 2.0 * math.log2(math.e) / width
    factor = 2.0 / width
    shape = jax.ShapeDtypeStruct

    arrays = (curve_embed, solution, targets, lengths.reshape(1, own), epoch_kernel)
    packed, columns, observed = pl.pallas_call(
        functools.partial(head_kernel, width),
        out_shape=(
            shape((own, width + 2 * epochs), BF16),
            shape((own, width + epochs), BF16),
            shape((own, epochs), BF16),
        ),
        in_specs=[pl.BlockSpec(memory_space=pltpu.HBM)] * 5,
        out_specs=[VMEM] * 3,
        scratch_shapes=[
            *(pltpu.VMEM(array.shape, array.dtype) for array in arrays),
            pltpu.SemaphoreType.DMA((5,)),
        ],
    )(*arrays)
    ids, halves = [slot_curve.reshape(1, own)], [observed]
    step = rows_axis // 2
    if step > 1:
        other = swap(packed, "row", step)
        columns = jnp.concatenate([columns, other[:, : width + epochs]], axis=0)
        observed = pl.pallas_call(
            functools.partial(observed_kernel, width + epochs),
            out_shape=shape((2 * own, epochs), BF16),
            in_specs=[VMEM] * 2,
            out_specs=VMEM,
            compiler_params=PARAMS,
            cost_estimate=pl.CostEstimate(
                flops=1 << 30, bytes_accessed=other.nbytes, transcendentals=0
            ),
        )(observed, other)
        halves, step = [observed], step // 2
    turn = 2
    while turn < cols_axis:
        ids += [swap(array, "col", turn) for array in ids]
        turn *= 2
    while step > 1:
        columns, halves = joined(columns, "row", step), [observed, swap(observed, "row", step)]
        step //= 2
        if step > 1:
            observed = jnp.concatenate(halves, axis=0)
    near = lax.all_gather(columns, "col", axis=0, tiled=True)
    near, halves, ids = lax.optimization_barrier((near, halves, ids))
    observed = jnp.concatenate(halves, axis=0)
    far = swap(near, "row", 1)
    observed = [observed]
    turn = 2
    while turn < cols_axis:
        observed += [swap(array, "col", turn) for array in observed]
        turn *= 2
    parts, half, chunk = len(ids), near.shape[0], columns.shape[0]
    held = parts * chunk
    cost = pl.CostEstimate(
        flops=2 * held * half * (2 * width + epochs),
        bytes_accessed=2 << 20,
        transcendentals=held * half,
    )
    kernels = (shape((parts * own, half), F32), shape((2 * own, held), F32))
    left, fit, *near_kernels = pl.pallas_call(
        functools.partial(near_kernel, scale, chunk, own),
        out_shape=(shape((held, 2 * width), BF16), shape((held, epochs), F32), *kernels),
        in_specs=[VMEM],
        out_specs=[VMEM] * 4,
        scratch_shapes=[pltpu.VMEM((half, 2 * width), BF16)],
        compiler_params=PARAMS,
        cost_estimate=cost,
    )(near)
    fit, *far_kernels = pl.pallas_call(
        functools.partial(far_kernel, scale, chunk, own),
        out_shape=(shape((held, epochs), F32), *kernels),
        in_specs=[VMEM] * 3,
        out_specs=[VMEM] * 3,
        scratch_shapes=[pltpu.VMEM((half, 2 * width), BF16)],
        compiler_params=PARAMS,
        cost_estimate=cost,
    )(far, left, fit)
    adjoint, col_far = pl.pallas_call(
        functools.partial(adjoint_kernel, factor, own),
        out_shape=(shape((held, epochs), BF16), shape((2 * own, width), F32)),
        in_specs=[VMEM] * (4 + parts),
        out_specs=[VMEM] * 2,
        compiler_params=PARAMS,
    )(far, left, fit, far_kernels[1], *observed)
    col_other = swap(col_far, "row", 1)
    col_near, row_part = pl.pallas_call(
        functools.partial(last_kernel, factor, chunk, parts, own),
        out_shape=(shape((2 * own, width), F32),) * 2,
        in_specs=[VMEM] * (7 + parts),
        out_specs=[VMEM] * 2,
        compiler_params=PARAMS,
        cost_estimate=cost,
    )(near, far, left, adjoint, *near_kernels, far_kernels[0], *ids)
    col_part = col_near + col_other
    other = swap(jnp.concatenate([col_part[own:], row_part[own:]], axis=0), "col", 1)
    return row_part[:own] + other[own:], col_part[:own] + other[:own]


def kernel_block(row_embed, row_square, piece_embed):
    piece_wide = piece_embed.astype(jnp.float32)
    products = lax.dot_general(
        row_embed, piece_embed, (((1,), (1,)), ((), ())), preferred_element_type=jnp.float32
    )
    distance = (
        row_square[:, None] + jnp.sum(piece_wide * piece_wide, axis=1)[None, :] - 2.0 * products
    )
    return jnp.exp(-distance / row_embed.shape[1])


def block_width():
    return 256


def make_fit(row_embed, row_square):

    def fit_fold(summed, pieces, offset):
        piece_embed, piece_fitted = pieces
        extent = piece_embed.shape[0]
        width_blk = block_width()

        def fit_advance(position, running):
            embed_part = lax.dynamic_slice_in_dim(piece_embed, position * width_blk, width_blk, 0)
            fitted_part = lax.dynamic_slice_in_dim(piece_fitted, position * width_blk, width_blk, 0)
            kernel = kernel_block(row_embed, row_square, embed_part).astype(jnp.bfloat16)
            return running + jnp.dot(kernel, fitted_part, preferred_element_type=jnp.float32)

        return lax.fori_loop(0, extent // width_blk, fit_advance, summed)

    return fit_fold


def make_grad(row_embed, row_square, row_wide, adjoint):

    def grad_fold(carry, pieces, offset):
        piece_embed, piece_fitted = pieces
        extent = piece_embed.shape[0]
        width_blk = block_width()

        def grad_advance(position, running):
            row_part, col_part = running
            embed_part = lax.dynamic_slice_in_dim(piece_embed, position * width_blk, width_blk, 0)
            fitted_part = lax.dynamic_slice_in_dim(piece_fitted, position * width_blk, width_blk, 0)
            kernel = kernel_block(row_embed, row_square, embed_part)
            link = lax.dot_general(
                adjoint, fitted_part, (((1,), (1,)), ((), ())), preferred_element_type=jnp.float32
            )
            weight = (link * kernel).astype(jnp.bfloat16)
            across = (
                jnp.dot(weight, embed_part, preferred_element_type=jnp.float32)
                - row_wide * jnp.sum(weight, axis=1, dtype=jnp.float32)[:, None]
            )
            down = lax.dot_general(
                weight, row_embed, (((0,), (0,)), ((), ())), preferred_element_type=jnp.float32
            )
            down = (
                down
                - embed_part.astype(jnp.float32)
                * jnp.sum(weight, axis=0, dtype=jnp.float32)[:, None]
            )
            first_row = offset + position * width_blk
            col_part = lax.dynamic_update_slice_in_dim(col_part, down, first_row, 0)
            return (row_part + across, col_part)

        return lax.fori_loop(0, extent // width_blk, grad_advance, carry)

    return grad_fold


def tiled_plan(curve_embed, solution, targets, lengths, slot_curve, epoch_kernel):
    own_rows = curve_embed.shape[0]
    width = curve_embed.shape[1]
    epochs_count = solution.shape[1]
    group_size = own_rows * lax.axis_size("col")
    column_size = own_rows * lax.axis_size("row")
    fitted_own = jnp.dot(
        solution, epoch_kernel, precision=lax.Precision.HIGHEST, preferred_element_type=jnp.float32
    ).astype(jnp.bfloat16)
    row_embed, row_curve = (
        lax.all_gather(curve_embed, "col", axis=0, tiled=True),
        lax.all_gather(slot_curve, "col", axis=0, tiled=True),
    )
    row_wide = row_embed.astype(jnp.float32)
    row_square = jnp.sum(row_wide * row_wide, axis=1)
    fit_fold = make_fit(row_embed, row_square)
    start_fit = jnp.zeros((group_size, epochs_count), jnp.float32)
    col_embed, col_fitted = (
        lax.all_gather(curve_embed, "row", axis=0, tiled=True),
        lax.all_gather(fitted_own, "row", axis=0, tiled=True),
    )
    fitted_sum = fit_fold(start_fit, (col_embed, col_fitted), 0)
    epochs = jnp.arange(epochs_count, dtype=jnp.int32)
    fitted_mine = lax.psum_scatter(fitted_sum, "col", scatter_dimension=0, tiled=True)
    observed = epochs[None, :] < lengths[:, None]
    adjoint_own = jnp.where(observed, targets.astype(jnp.float32) - fitted_mine, 0.0).astype(
        jnp.bfloat16
    )
    adjoint = lax.all_gather(adjoint_own, "col", axis=0, tiled=True)
    grad_fold = make_grad(row_embed, row_square, row_wide, adjoint)
    start_grad = (
        jnp.zeros((group_size, width), jnp.float32),
        jnp.zeros((column_size, width), jnp.float32),
    )
    row_sum, col_sum = grad_fold(start_grad, (col_embed, col_fitted), 0)
    group_base = lax.axis_index("row") * group_size
    local_curve = (row_curve - group_base).astype(jnp.int32)
    inverse = (
        jnp.zeros((group_size,), jnp.int32)
        .at[local_curve]
        .set(jnp.arange(group_size, dtype=jnp.int32))
    )
    reordered = jnp.take(row_sum, inverse, axis=0)
    factor = 2.0 / width
    row_grad = lax.psum_scatter(reordered, "col", scatter_dimension=0, tiled=True) * factor
    col_grad = lax.psum_scatter(col_sum, "row", scatter_dimension=0, tiled=True) * factor
    return (row_grad, col_grad)


def power_of_two(number):
    return number >= 2 and number & (number - 1) == 0


def per_device(curve_embed, solution, *rest):
    own, width = curve_embed.shape
    rows_axis, cols_axis = lax.axis_size("row"), lax.axis_size("col")
    gathered = own * rows_axis * cols_axis * (width + solution.shape[1]) * 2
    if gathered <= GATHER_LIMIT and power_of_two(rows_axis) and power_of_two(cols_axis):
        return gathered_plan(curve_embed, solution, *rest)
    return tiled_plan(curve_embed, solution, *rest)


def solution(mesh):
    in_specs = (
        P(("row", "col"), None),
        P(("row", "col"), None),
        P(("row", "col"), None),
        P(("row", "col")),
        P(("row", "col")),
        P(),
    )
    out_specs = (P(("row", "col"), None), P(("row", "col"), None))
    return jax.shard_map(
        per_device, mesh=mesh, in_specs=in_specs, out_specs=out_specs, check_vma=False
    )
```

```python
import functools
import math

import jax
import jax.numpy as jnp
from jax import lax
from jax.experimental import pallas as pl
from jax.experimental.pallas import tpu as pltpu
from jax.sharding import PartitionSpec as P

GATHER_LIMIT = 4 << 20
BF16, F32 = jnp.bfloat16, jnp.float32
VMEM = pl.BlockSpec(memory_space=pltpu.VMEM)
SMEM = pl.BlockSpec(memory_space=pltpu.SMEM)
PARAMS = pltpu.CompilerParams(vmem_limit_bytes=24 << 20)


def nt_dot(left, right):
    return lax.dot_general(left, right, (((1,), (1,)), ((), ())), preferred_element_type=F32)


def nn_dot(left, right):
    return jnp.dot(left, right, preferred_element_type=F32)


def extended(embed):
    rows, width = embed.shape
    wide = embed.astype(F32)
    square = wide * wide
    high = square.astype(BF16)
    low = (square - high.astype(F32)).astype(BF16)
    ones = jnp.ones((2 * width, width), BF16)
    half = -0.5 * nn_dot(jnp.concatenate([high, low], axis=1), ones)
    first = half.astype(BF16).astype(F32)
    second = (half - first).astype(BF16).astype(F32)
    third = half - first - second
    lane = lax.broadcasted_iota(jnp.int32, (rows, width), 1)

    def lanes(at, one_at):
        tail = jnp.where((lane >= one_at) & (lane < one_at + 3), 1.0, 0.0)
        for offset, term in enumerate((first, second, third)):
            tail = jnp.where(lane == at + offset, term, tail)
        return jnp.concatenate([embed, tail.astype(BF16)], axis=1)

    return lanes


def head_kernel(width, *refs):
    out_ref, columns_ref, observed_ref = refs[5:8]
    held, semaphores = refs[8:13], refs[13]
    copies = [
        pltpu.make_async_copy(source, target, semaphores.at[index])
        for index, (source, target) in enumerate(zip(refs[:5], held))
    ]
    for copy in copies:
        copy.start()
    for copy in copies:
        copy.wait()
    embed_ref, solution_ref, targets_ref, lengths_ref, epoch_ref = held
    rows, epochs = solution_ref.shape
    fitted = jnp.dot(
        solution_ref[...], epoch_ref[...], precision=lax.Precision.HIGHEST, preferred_element_type=F32
    )
    row = lax.broadcasted_iota(jnp.int32, (rows, rows), 0)
    column = lax.broadcasted_iota(jnp.int32, (rows, rows), 1)
    lengths = jnp.sum(
        jnp.where(row == column, lengths_ref[...], 0).astype(F32), axis=1, keepdims=True
    )
    epoch = lax.broadcasted_iota(jnp.int32, (rows, epochs), 1).astype(F32)
    targets = jnp.where(epoch < lengths, targets_ref[...].astype(F32), jnp.inf)
    columns = jnp.concatenate([embed_ref[...], fitted.astype(BF16)], axis=1)
    columns_ref[...] = columns
    observed_ref[...] = targets.astype(BF16)
    out_ref[:, : width + epochs] = columns
    out_ref[:, width + epochs :] = targets.astype(BF16)


def observed_kernel(first, own_ref, other_ref, out_ref):
    out_ref[: own_ref.shape[0], :] = own_ref[...]
    out_ref[own_ref.shape[0] :, :] = other_ref[:, first:]


def with_ones(embed):
    return jnp.concatenate([embed, jnp.ones_like(embed)], axis=1)


def gradient(factor, summed, embed):
    width = embed.shape[1]
    return factor * (summed[:, :width] - embed.astype(F32) * summed[:, width:])


def stacked(refs, rows):
    return jnp.concatenate([ref[:rows, :] for ref in refs], axis=0)


def slot_runs(ref, own):
    half = ref.shape[0] // 2
    return jnp.concatenate([ref[:own, :], ref[half : half + own, :]], axis=0)


def fit_part(scale, own, columns_refs, left_ref, slots_ref, total):
    width = left_ref.shape[1] // 2
    left = left_ref[...]
    slots_left = slot_runs(left_ref, own)
    place = 0
    for ref in columns_refs:
        block = ref.shape[0]
        right = extended(ref[:, :width])(0, 3)
        kernel = jnp.exp2(nt_dot(left, right) * scale).astype(BF16)
        part = nn_dot(kernel, ref[:, width:])
        total = part if total is None else total + part
        slots_ref[:, place : place + block] = jnp.exp2(nt_dot(slots_left, right) * scale)
        place += block
    return total


def pick_kernels(scale, own, first_ref, second_ref, left_ref, picks_ref):
    width = left_ref.shape[1] // 2
    right = extended(stacked((first_ref, second_ref), own)[:, :width])(0, 3)
    picks_ref[...] = jnp.exp2(nt_dot(right, left_ref[...]) * scale)


def near_kernel(scale, own, own_ref, x_ref, y_ref, left_ref, fit_ref, slots_ref, picks_ref):
    block, width = own_ref.shape[0], left_ref.shape[1] // 2
    for part, ref in enumerate((own_ref, y_ref)):
        left_ref[part * block : (part + 1) * block, :] = extended(ref[:, :width])(3, 0)
    columns = (own_ref, x_ref, y_ref)
    fit_ref[...] = fit_part(scale, own, columns, left_ref, slots_ref, None)
    pick_kernels(scale, own, own_ref, x_ref, left_ref, picks_ref)


def far_kernel(scale, own, *refs):
    own_ref, x_ref, y_ref, left_ref, before_ref, fit_ref, slots_ref, picks_ref = refs
    columns = (own_ref, x_ref, y_ref)
    fit_ref[...] = fit_part(scale, own, columns, left_ref, slots_ref, before_ref[...])
    pick_kernels(scale, own, own_ref, x_ref, left_ref, picks_ref)


def across_kernel(scale, own, *refs):
    columns, (left_ref, before_ref, fit_ref, slots_ref) = refs[:2], refs[2:]
    fit_ref[...] = fit_part(scale, own, columns, left_ref, slots_ref, before_ref[...])


def column_part(factor, own, adjoint, embed, refs, kernel_ref):
    width = embed.shape[1]
    columns = stacked(refs, own)
    weight = (nt_dot(columns[:, width:], adjoint) * kernel_ref[...]).astype(BF16)
    return gradient(factor, nn_dot(weight, with_ones(embed)), columns[:, :width])


def adjoint_kernel(scale, factor, own, *refs):
    columns, (left_ref, before_ref, own_ref, x_ref, picks_ref) = refs[:2], refs[2:7]
    targets_refs, (slots_ref, adjoint_ref, col_ref) = refs[7:9], refs[9:]
    width = left_ref.shape[1] // 2
    block = left_ref.shape[0] // 2
    fit = fit_part(scale, own, columns, left_ref, slots_ref, before_ref[...])
    for part, targets_ref in enumerate(targets_refs):
        span = slice(part * block, (part + 1) * block)
        targets = targets_ref[...].astype(F32)
        adjoint = jnp.where(targets == jnp.inf, 0.0, targets - fit[span])
        adjoint_ref[span, :] = adjoint.astype(BF16)
    col_ref[...] = column_part(
        factor, own, adjoint_ref[...], left_ref[:, :width], (own_ref, x_ref), picks_ref
    )


def last_kernel(factor, own, *refs):
    columns_refs, slots_refs = refs[:10], refs[10:14]
    left_ref, adjoint_ref, picks_ref = refs[14:17]
    ids_refs, (col_ref, row_ref) = refs[17:19], refs[19:]
    width = left_ref.shape[1] // 2
    col_ref[...] = column_part(
        factor, own, adjoint_ref[...], left_ref[:, :width], columns_refs[:2], picks_ref
    )
    slots_embed = slot_runs(left_ref, own)[:, :width]
    slots_adjoint = slot_runs(adjoint_ref, own)
    half = columns_refs[-1].shape[0]
    places = [(ref, at) for ref in slots_refs for at in range(0, ref.shape[1], half)]
    summed = None
    for ref in columns_refs:
        link = nt_dot(slots_adjoint, ref[:, width:])
        kernel = []
        for _ in range(ref.shape[0] // half):
            kernel_ref, at = places.pop(0)
            kernel.append(kernel_ref[:, at : at + half])
        weight = (link * jnp.concatenate(kernel, axis=1)).astype(BF16)
        part = nn_dot(weight, with_ones(ref[:, :width]))
        summed = part if summed is None else summed + part
    slot_rows = gradient(factor, summed, slots_embed)
    ids = jnp.concatenate([jnp.broadcast_to(ref[...], (own, own)) for ref in ids_refs], axis=1)
    wanted = lax.broadcasted_iota(jnp.int32, ids.shape, 0)
    first = lax.axis_index("row") * lax.axis_size("col")
    for mask in (0, 1):
        base = (first + (lax.axis_index("col") ^ mask)) * own
        chosen = (ids == wanted + base).astype(F32)
        row_ref[mask * own : (mask + 1) * own, :] = jnp.dot(
            chosen, slot_rows, precision=lax.Precision.HIGHEST, preferred_element_type=F32
        )


def observed_kernel(first, own_ref, other_ref, out_ref):
    out_ref[: own_ref.shape[0], :] = own_ref[...]
    out_ref[own_ref.shape[0] :, :] = other_ref[:, first:]


def swap(array, axis, mask):
    pairs = [(index, index ^ mask) for index in range(lax.axis_size(axis))]
    return lax.ppermute(array, axis, pairs)


def joined(array, axis, mask):
    return jnp.concatenate([array, swap(array, axis, mask)], axis=0)


def gathered_plan(curve_embed, solution, targets, lengths, slot_curve, epoch_kernel):
    own, width = curve_embed.shape
    epochs = solution.shape[1]
    rows_axis, cols_axis = lax.axis_size("row"), lax.axis_size("col")
    scale = 2.0 * math.log2(math.e) / width
    factor = 2.0 / width
    shape = jax.ShapeDtypeStruct

    arrays = (curve_embed, solution, targets, lengths.reshape(1, own), epoch_kernel)
    packed, columns, observed = pl.pallas_call(
        functools.partial(head_kernel, width),
        out_shape=(
            shape((own, width + 2 * epochs), BF16),
            shape((own, width + epochs), BF16),
            shape((own, epochs), BF16),
        ),
        in_specs=[pl.BlockSpec(memory_space=pltpu.HBM)] * 5,
        out_specs=[VMEM] * 3,
        scratch_shapes=[
            *(pltpu.VMEM(array.shape, array.dtype) for array in arrays),
            pltpu.SemaphoreType.DMA((5,)),
        ],
    )(*arrays)
    ids, halves = [slot_curve.reshape(1, own)], [observed]
    step = rows_axis // 2
    if step > 1:
        other = swap(packed, "row", step)
        columns = jnp.concatenate([columns, other[:, : width + epochs]], axis=0)
        observed = pl.pallas_call(
            functools.partial(observed_kernel, width + epochs),
            out_shape=shape((2 * own, epochs), BF16),
            in_specs=[VMEM] * 2,
            out_specs=VMEM,
            compiler_params=PARAMS,
            cost_estimate=pl.CostEstimate(
                flops=1 << 30, bytes_accessed=other.nbytes, transcendentals=0
            ),
        )(observed, other)
        halves, step = [observed], step // 2
    ids.append(swap(ids[0], "col", 2))
    while step > 1:
        columns, halves = joined(columns, "row", step), [observed, swap(observed, "row", step)]
        step //= 2
        if step > 1:
            observed = jnp.concatenate(halves, axis=0)
    block = columns.shape[0]
    held, half = 2 * block, block // 2
    x_block, y_block = swap(columns, "col", 1), swap(columns, "col", 2)
    across = (swap(x_block[:half], "col", 2), swap(y_block[half:], "col", 1))
    near = (columns, x_block, y_block)
    far = tuple(swap(array, "row", 1) for array in near)

    def call(body, outs, *inputs):
        blocks = 3 if body in (near_kernel, far_kernel) else 1
        return pl.pallas_call(
            functools.partial(body, scale, own),
            out_shape=outs,
            in_specs=[VMEM] * len(inputs),
            out_specs=[VMEM] * len(outs),
            compiler_params=PARAMS,
            cost_estimate=pl.CostEstimate(
                flops=2 * held * blocks * block * (2 * width + epochs),
                bytes_accessed=1 << 20,
                transcendentals=held * blocks * block,
            ),
        )(*inputs)

    fit_shape, picks_shape = shape((held, epochs), F32), shape((2 * own, held), F32)
    slots = [shape((2 * own, count * block), F32) for count in (3, 1)]
    left, fit, slots_near, picks_near = call(
        near_kernel,
        (shape((held, 2 * width), BF16), fit_shape, slots[0], picks_shape),
        *near,
    )
    fit, halves, ids = lax.optimization_barrier((fit, halves, ids))
    observed = jnp.concatenate(halves, axis=0)
    observed_y = swap(observed, "col", 2)
    fit, slots_far, picks_far = call(
        far_kernel, (fit_shape, slots[0], picks_shape), *far, left, fit
    )
    across, fit = lax.optimization_barrier((across, fit))
    far_across = tuple(swap(array, "row", 1) for array in across)
    fit, slots_across = call(across_kernel, (fit_shape, slots[1]), *across, left, fit)
    slots_last, adjoint, col_far = pl.pallas_call(
        functools.partial(adjoint_kernel, scale, factor, own),
        out_shape=(slots[1], shape((held, epochs), BF16), shape((2 * own, width), F32)),
        in_specs=[VMEM] * 9,
        out_specs=[VMEM] * 3,
        compiler_params=PARAMS,
    )(*far_across, left, fit, *far[:2], picks_far, observed, observed_y)
    col_other = swap(col_far, "row", 1)
    col_near, row_part = pl.pallas_call(
        functools.partial(last_kernel, factor, own),
        out_shape=(shape((2 * own, width), F32),) * 2,
        in_specs=[VMEM] * 19,
        out_specs=[VMEM] * 2,
        compiler_params=PARAMS,
        cost_estimate=pl.CostEstimate(flops=1 << 29, bytes_accessed=1 << 20, transcendentals=0),
    )(
        *(*near, *far, *across, *far_across),
        *(slots_near, slots_far, slots_across, slots_last),
        *(left, adjoint, picks_near, *ids),
    )
    col_part = col_near + col_other
    other = swap(jnp.concatenate([col_part[own:], row_part[own:]], axis=0), "col", 1)
    return row_part[:own] + other[own:], col_part[:own] + other[:own]


def kernel_block(row_embed, row_square, piece_embed):
    piece_wide = piece_embed.astype(jnp.float32)
    products = lax.dot_general(
        row_embed, piece_embed, (((1,), (1,)), ((), ())), preferred_element_type=jnp.float32
    )
    distance = (
        row_square[:, None] + jnp.sum(piece_wide * piece_wide, axis=1)[None, :] - 2.0 * products
    )
    return jnp.exp(-distance / row_embed.shape[1])


def block_width():
    return 256


def make_fit(row_embed, row_square):

    def fit_fold(summed, pieces, offset):
        piece_embed, piece_fitted = pieces
        extent = piece_embed.shape[0]
        width_blk = block_width()

        def fit_advance(position, running):
            embed_part = lax.dynamic_slice_in_dim(piece_embed, position * width_blk, width_blk, 0)
            fitted_part = lax.dynamic_slice_in_dim(piece_fitted, position * width_blk, width_blk, 0)
            kernel = kernel_block(row_embed, row_square, embed_part).astype(jnp.bfloat16)
            return running + jnp.dot(kernel, fitted_part, preferred_element_type=jnp.float32)

        return lax.fori_loop(0, extent // width_blk, fit_advance, summed)

    return fit_fold


def make_grad(row_embed, row_square, row_wide, adjoint):

    def grad_fold(carry, pieces, offset):
        piece_embed, piece_fitted = pieces
        extent = piece_embed.shape[0]
        width_blk = block_width()

        def grad_advance(position, running):
            row_part, col_part = running
            embed_part = lax.dynamic_slice_in_dim(piece_embed, position * width_blk, width_blk, 0)
            fitted_part = lax.dynamic_slice_in_dim(piece_fitted, position * width_blk, width_blk, 0)
            kernel = kernel_block(row_embed, row_square, embed_part)
            link = lax.dot_general(
                adjoint, fitted_part, (((1,), (1,)), ((), ())), preferred_element_type=jnp.float32
            )
            weight = (link * kernel).astype(jnp.bfloat16)
            across = (
                jnp.dot(weight, embed_part, preferred_element_type=jnp.float32)
                - row_wide * jnp.sum(weight, axis=1, dtype=jnp.float32)[:, None]
            )
            down = lax.dot_general(
                weight, row_embed, (((0,), (0,)), ((), ())), preferred_element_type=jnp.float32
            )
            down = (
                down
                - embed_part.astype(jnp.float32)
                * jnp.sum(weight, axis=0, dtype=jnp.float32)[:, None]
            )
            first_row = offset + position * width_blk
            col_part = lax.dynamic_update_slice_in_dim(col_part, down, first_row, 0)
            return (row_part + across, col_part)

        return lax.fori_loop(0, extent // width_blk, grad_advance, carry)

    return grad_fold


def tiled_plan(curve_embed, solution, targets, lengths, slot_curve, epoch_kernel):
    own_rows = curve_embed.shape[0]
    width = curve_embed.shape[1]
    epochs_count = solution.shape[1]
    group_size = own_rows * lax.axis_size("col")
    column_size = own_rows * lax.axis_size("row")
    fitted_own = jnp.dot(
        solution, epoch_kernel, precision=lax.Precision.HIGHEST, preferred_element_type=jnp.float32
    ).astype(jnp.bfloat16)
    row_embed, row_curve = (
        lax.all_gather(curve_embed, "col", axis=0, tiled=True),
        lax.all_gather(slot_curve, "col", axis=0, tiled=True),
    )
    row_wide = row_embed.astype(jnp.float32)
    row_square = jnp.sum(row_wide * row_wide, axis=1)
    fit_fold = make_fit(row_embed, row_square)
    start_fit = jnp.zeros((group_size, epochs_count), jnp.float32)
    col_embed, col_fitted = (
        lax.all_gather(curve_embed, "row", axis=0, tiled=True),
        lax.all_gather(fitted_own, "row", axis=0, tiled=True),
    )
    fitted_sum = fit_fold(start_fit, (col_embed, col_fitted), 0)
    epochs = jnp.arange(epochs_count, dtype=jnp.int32)
    fitted_mine = lax.psum_scatter(fitted_sum, "col", scatter_dimension=0, tiled=True)
    observed = epochs[None, :] < lengths[:, None]
    adjoint_own = jnp.where(observed, targets.astype(jnp.float32) - fitted_mine, 0.0).astype(
        jnp.bfloat16
    )
    adjoint = lax.all_gather(adjoint_own, "col", axis=0, tiled=True)
    grad_fold = make_grad(row_embed, row_square, row_wide, adjoint)
    start_grad = (
        jnp.zeros((group_size, width), jnp.float32),
        jnp.zeros((column_size, width), jnp.float32),
    )
    row_sum, col_sum = grad_fold(start_grad, (col_embed, col_fitted), 0)
    group_base = lax.axis_index("row") * group_size
    local_curve = (row_curve - group_base).astype(jnp.int32)
    inverse = (
        jnp.zeros((group_size,), jnp.int32)
        .at[local_curve]
        .set(jnp.arange(group_size, dtype=jnp.int32))
    )
    reordered = jnp.take(row_sum, inverse, axis=0)
    factor = 2.0 / width
    row_grad = lax.psum_scatter(reordered, "col", scatter_dimension=0, tiled=True) * factor
    col_grad = lax.psum_scatter(col_sum, "row", scatter_dimension=0, tiled=True) * factor
    return (row_grad, col_grad)


def power_of_two(number):
    return number >= 2 and number & (number - 1) == 0


def per_device(curve_embed, solution, *rest):
    own, width = curve_embed.shape
    rows_axis, cols_axis = lax.axis_size("row"), lax.axis_size("col")
    gathered = own * rows_axis * cols_axis * (width + solution.shape[1]) * 2
    if gathered <= GATHER_LIMIT and power_of_two(rows_axis) and cols_axis == 4:
        return gathered_plan(curve_embed, solution, *rest)
    return tiled_plan(curve_embed, solution, *rest)


def solution(mesh):
    in_specs = (
        P(("row", "col"), None),
        P(("row", "col"), None),
        P(("row", "col"), None),
        P(("row", "col")),
        P(("row", "col")),
        P(),
    )
    out_specs = (P(("row", "col"), None), P(("row", "col"), None))
    return jax.shard_map(
        per_device, mesh=mesh, in_specs=in_specs, out_specs=out_specs, check_vma=False
    )
```

```python
import functools
import math

import jax
import jax.numpy as jnp
from jax import lax
from jax.experimental import pallas as pl
from jax.experimental.pallas import tpu as pltpu
from jax.sharding import PartitionSpec as P

GATHER_LIMIT = 4 << 20
BF16, F32 = jnp.bfloat16, jnp.float32
VMEM = pl.BlockSpec(memory_space=pltpu.VMEM)
SMEM = pl.BlockSpec(memory_space=pltpu.SMEM)
PARAMS = pltpu.CompilerParams(vmem_limit_bytes=24 << 20)


def nt_dot(left, right):
    return lax.dot_general(left, right, (((1,), (1,)), ((), ())), preferred_element_type=F32)


def nn_dot(left, right):
    return jnp.dot(left, right, preferred_element_type=F32)


def extended(embed):
    rows, width = embed.shape
    wide = embed.astype(F32)
    square = wide * wide
    high = square.astype(BF16)
    low = (square - high.astype(F32)).astype(BF16)
    ones = jnp.ones((2 * width, width), BF16)
    half = -0.5 * nn_dot(jnp.concatenate([high, low], axis=1), ones)
    first = half.astype(BF16).astype(F32)
    second = (half - first).astype(BF16).astype(F32)
    third = half - first - second
    lane = lax.broadcasted_iota(jnp.int32, (rows, width), 1)

    def lanes(at, one_at):
        tail = jnp.where((lane >= one_at) & (lane < one_at + 3), 1.0, 0.0)
        for offset, term in enumerate((first, second, third)):
            tail = jnp.where(lane == at + offset, term, tail)
        return jnp.concatenate([embed, tail.astype(BF16)], axis=1)

    return lanes


def head_kernel(width, *refs):
    out_ref, columns_ref, observed_ref = refs[5:8]
    held, semaphores = refs[8:13], refs[13]
    copies = [
        pltpu.make_async_copy(source, target, semaphores.at[index])
        for index, (source, target) in enumerate(zip(refs[:5], held))
    ]
    for copy in copies:
        copy.start()
    for copy in copies:
        copy.wait()
    embed_ref, solution_ref, targets_ref, lengths_ref, epoch_ref = held
    rows, epochs = solution_ref.shape
    fitted = jnp.dot(
        solution_ref[...], epoch_ref[...], precision=lax.Precision.HIGHEST, preferred_element_type=F32
    )
    row = lax.broadcasted_iota(jnp.int32, (rows, rows), 0)
    column = lax.broadcasted_iota(jnp.int32, (rows, rows), 1)
    lengths = jnp.sum(
        jnp.where(row == column, lengths_ref[...], 0).astype(F32), axis=1, keepdims=True
    )
    epoch = lax.broadcasted_iota(jnp.int32, (rows, epochs), 1).astype(F32)
    targets = jnp.where(epoch < lengths, targets_ref[...].astype(F32), jnp.inf)
    columns = jnp.concatenate([embed_ref[...], fitted.astype(BF16)], axis=1)
    columns_ref[...] = columns
    observed_ref[...] = targets.astype(BF16)
    out_ref[:, : width + epochs] = columns
    out_ref[:, width + epochs :] = targets.astype(BF16)


def observed_kernel(first, own_ref, other_ref, out_ref):
    out_ref[: own_ref.shape[0], :] = own_ref[...]
    out_ref[own_ref.shape[0] :, :] = other_ref[:, first:]


def with_ones(embed):
    return jnp.concatenate([embed, jnp.ones_like(embed)], axis=1)


def gradient(factor, summed, embed):
    width = embed.shape[1]
    return factor * (summed[:, :width] - embed.astype(F32) * summed[:, width:])


def stacked(refs, rows):
    return jnp.concatenate([ref[:rows, :] for ref in refs], axis=0)


def slot_runs(ref, own):
    half = ref.shape[0] // 2
    return jnp.concatenate([ref[:own, :], ref[half : half + own, :]], axis=0)


def joint(refs):
    return jnp.concatenate([ref[...] for ref in refs], axis=0)


def fit_part(scale, own, groups, left_ref, slots_ref, total):
    width = left_ref.shape[1] // 2
    left = left_ref[...]
    slots_left = slot_runs(left_ref, own)
    place = 0
    for group in groups:
        columns = joint(group)
        right = extended(columns[:, :width])(0, 3)
        kernel = jnp.exp2(nt_dot(left, right) * scale).astype(BF16)
        part = nn_dot(kernel, columns[:, width:])
        total = part if total is None else total + part
        slots_ref[:, place : place + columns.shape[0]] = jnp.exp2(
            nt_dot(slots_left, right) * scale
        )
        place += columns.shape[0]
    return total


def pick_kernels(scale, own, first_ref, second_ref, left_ref, picks_ref):
    width = left_ref.shape[1] // 2
    right = extended(stacked((first_ref, second_ref), own)[:, :width])(0, 3)
    picks_ref[...] = jnp.exp2(nt_dot(right, left_ref[...]) * scale)


def main_kernel(scale, own, *refs):
    near, far = [refs[:2], refs[2:4], refs[4:6]], [(ref,) for ref in refs[6:9]]
    left_ref, fit_ref, slots_ref, near_picks_ref, far_picks_ref = refs[9:]
    block, width = left_ref.shape[0] // 2, left_ref.shape[1] // 2
    for part, group in enumerate((near[0], near[2])):
        left_ref[part * block : (part + 1) * block, :] = extended(joint(group)[:, :width])(3, 0)
    fit_ref[...] = fit_part(scale, own, near + far, left_ref, slots_ref, None)
    pick_kernels(scale, own, refs[0], refs[2], left_ref, near_picks_ref)
    pick_kernels(scale, own, refs[6], refs[7], left_ref, far_picks_ref)


def across_kernel(scale, own, *refs):
    group, (left_ref, before_ref, fit_ref, slots_ref) = refs[:2], refs[2:]
    fit_ref[...] = fit_part(scale, own, (group,), left_ref, slots_ref, before_ref[...])


def column_part(factor, own, adjoint, embed, refs, kernel_ref):
    width = embed.shape[1]
    columns = stacked(refs, own)
    weight = (nt_dot(columns[:, width:], adjoint) * kernel_ref[...]).astype(BF16)
    return gradient(factor, nn_dot(weight, with_ones(embed)), columns[:, :width])


def adjoint_kernel(scale, factor, own, *refs):
    group, (left_ref, before_ref, own_ref, x_ref, picks_ref) = refs[:2], refs[2:7]
    first_ref, first_y_ref, second_ref, slots_ref, adjoint_ref, col_ref = refs[7:]
    width = left_ref.shape[1] // 2
    half = first_ref.shape[0]
    fit = fit_part(scale, own, (group,), left_ref, slots_ref, before_ref[...])
    targets = (first_ref[...], second_ref[:half, :], first_y_ref[...], second_ref[half:, :])
    for part, values in enumerate(targets):
        span = slice(part * half, (part + 1) * half)
        values = values.astype(F32)
        adjoint = jnp.where(values == jnp.inf, 0.0, values - fit[span])
        adjoint_ref[span, :] = adjoint.astype(BF16)
    col_ref[...] = column_part(
        factor, own, adjoint_ref[...], left_ref[:, :width], (own_ref, x_ref), picks_ref
    )


def last_kernel(factor, own, *refs):
    groups = [refs[at : at + 2] for at in (0, 2, 4)]
    groups += [refs[at : at + 1] for at in (6, 7, 8)] + [refs[9:11], refs[11:13]]
    slots_refs, (left_ref, adjoint_ref, picks_ref) = refs[13:16], refs[16:19]
    ids_refs, (col_ref, row_ref) = refs[19:21], refs[21:]
    width = left_ref.shape[1] // 2
    col_ref[...] = column_part(
        factor, own, adjoint_ref[...], left_ref[:, :width], (refs[0], refs[2]), picks_ref
    )
    slots_embed = slot_runs(left_ref, own)[:, :width]
    slots_adjoint = slot_runs(adjoint_ref, own)
    block = left_ref.shape[0] // 2
    places = [(ref, at) for ref in slots_refs for at in range(0, ref.shape[1], block)]
    summed = None
    for group, (kernel_ref, at) in zip(groups, places):
        columns = joint(group)
        link = nt_dot(slots_adjoint, columns[:, width:])
        weight = (link * kernel_ref[:, at : at + block]).astype(BF16)
        part = nn_dot(weight, with_ones(columns[:, :width]))
        summed = part if summed is None else summed + part
    slot_rows = gradient(factor, summed, slots_embed)
    ids = jnp.concatenate([jnp.broadcast_to(ref[...], (own, own)) for ref in ids_refs], axis=1)
    wanted = lax.broadcasted_iota(jnp.int32, ids.shape, 0)
    first = lax.axis_index("row") * lax.axis_size("col")
    for mask in (0, 1):
        base = (first + (lax.axis_index("col") ^ mask)) * own
        chosen = (ids == wanted + base).astype(F32)
        row_ref[mask * own : (mask + 1) * own, :] = jnp.dot(
            chosen, slot_rows, precision=lax.Precision.HIGHEST, preferred_element_type=F32
        )


def observed_kernel(first, own_ref, other_ref, out_ref):
    out_ref[: own_ref.shape[0], :] = own_ref[...]
    out_ref[own_ref.shape[0] :, :] = other_ref[:, first:]


def swap(array, axis, mask):
    pairs = [(index, index ^ mask) for index in range(lax.axis_size(axis))]
    return lax.ppermute(array, axis, pairs)


def joined(array, axis, mask):
    return jnp.concatenate([array, swap(array, axis, mask)], axis=0)


def gathered_plan(curve_embed, solution, targets, lengths, slot_curve, epoch_kernel):
    own, width = curve_embed.shape
    epochs = solution.shape[1]
    rows_axis, cols_axis = lax.axis_size("row"), lax.axis_size("col")
    scale = 2.0 * math.log2(math.e) / width
    factor = 2.0 / width
    shape = jax.ShapeDtypeStruct

    arrays = (curve_embed, solution, targets, lengths.reshape(1, own), epoch_kernel)
    packed, columns, observed = pl.pallas_call(
        functools.partial(head_kernel, width),
        out_shape=(
            shape((own, width + 2 * epochs), BF16),
            shape((own, width + epochs), BF16),
            shape((own, epochs), BF16),
        ),
        in_specs=[pl.BlockSpec(memory_space=pltpu.HBM)] * 5,
        out_specs=[VMEM] * 3,
        scratch_shapes=[
            *(pltpu.VMEM(array.shape, array.dtype) for array in arrays),
            pltpu.SemaphoreType.DMA((5,)),
        ],
    )(*arrays)
    ids = slot_curve.reshape(1, own)
    step = rows_axis // 2
    other, ids_y = lax.optimization_barrier((swap(packed, "row", step), swap(ids, "col", 2)))
    columns = jnp.concatenate([columns, other[:, : width + epochs]], axis=0)
    observed = pl.pallas_call(
        functools.partial(observed_kernel, width + epochs),
        out_shape=shape((2 * own, epochs), BF16),
        in_specs=[VMEM] * 2,
        out_specs=VMEM,
        compiler_params=PARAMS,
        cost_estimate=pl.CostEstimate(
            flops=1 << 30, bytes_accessed=other.nbytes, transcendentals=0
        ),
    )(observed, other)
    step //= 2
    while step > 2:
        columns, observed = joined(columns, "row", step), joined(observed, "row", step)
        step //= 2
    first, second = columns, swap(columns, "row", 2)
    x_first, y_first = swap(first, "col", 1), swap(first, "col", 2)
    y_second, x_second = swap(second, "col", 2), swap(second, "col", 1)
    near = (first, second, x_first, x_second, y_first, y_second)
    across = (swap(x_first, "col", 2), swap(y_second, "col", 1))
    far = tuple(
        swap(jnp.concatenate(near[at : at + 2], axis=0), "row", 1) for at in (0, 2, 4)
    )
    half = first.shape[0]
    block, held = 2 * half, 4 * half

    def call(body, outs, *inputs):
        return pl.pallas_call(
            functools.partial(body, scale, own),
            out_shape=outs,
            in_specs=[VMEM] * len(inputs),
            out_specs=[VMEM] * len(outs),
            compiler_params=PARAMS,
            cost_estimate=pl.CostEstimate(flops=1 << 16, bytes_accessed=1 << 10, transcendentals=0),
        )(*inputs)

    fit_shape, picks_shape = shape((held, epochs), F32), shape((2 * own, held), F32)
    slots = [shape((2 * own, count * block), F32) for count in (6, 1)]
    observed_pair = (observed, swap(observed, "col", 2))
    observed_z = swap(jnp.concatenate(observed_pair, axis=0), "row", 2)
    left, fit, slots_main, picks_near, picks_far = call(
        main_kernel,
        (shape((held, 2 * width), BF16), fit_shape, slots[0], picks_shape, picks_shape),
        *(*near, *far),
    )
    across, fit = lax.optimization_barrier((across, fit))
    far_across = tuple(swap(array, "row", 1) for array in across)
    fit, slots_across = call(across_kernel, (fit_shape, slots[1]), *across, left, fit)
    slots_last, adjoint, col_far = pl.pallas_call(
        functools.partial(adjoint_kernel, scale, factor, own),
        out_shape=(slots[1], shape((held, epochs), BF16), shape((2 * own, width), F32)),
        in_specs=[VMEM] * 10,
        out_specs=[VMEM] * 3,
        compiler_params=PARAMS,
    )(*far_across, left, fit, *far[:2], picks_far, *observed_pair, observed_z)
    col_other = swap(col_far, "row", 1)
    col_near, row_part = pl.pallas_call(
        functools.partial(last_kernel, factor, own),
        out_shape=(shape((2 * own, width), F32),) * 2,
        in_specs=[VMEM] * 21,
        out_specs=[VMEM] * 2,
        compiler_params=PARAMS,
        cost_estimate=pl.CostEstimate(flops=1 << 29, bytes_accessed=1 << 20, transcendentals=0),
    )(
        *(*near, *far, *across, *far_across),
        *(slots_main, slots_across, slots_last),
        *(left, adjoint, picks_near, ids, ids_y),
    )
    col_part = col_near + col_other
    other = swap(jnp.concatenate([col_part[own:], row_part[own:]], axis=0), "col", 1)
    return row_part[:own] + other[own:], col_part[:own] + other[:own]


def kernel_block(row_embed, row_square, piece_embed):
    piece_wide = piece_embed.astype(jnp.float32)
    products = lax.dot_general(
        row_embed, piece_embed, (((1,), (1,)), ((), ())), preferred_element_type=jnp.float32
    )
    distance = (
        row_square[:, None] + jnp.sum(piece_wide * piece_wide, axis=1)[None, :] - 2.0 * products
    )
    return jnp.exp(-distance / row_embed.shape[1])


def block_width():
    return 256


def make_fit(row_embed, row_square):

    def fit_fold(summed, pieces, offset):
        piece_embed, piece_fitted = pieces
        extent = piece_embed.shape[0]
        width_blk = block_width()

        def fit_advance(position, running):
            embed_part = lax.dynamic_slice_in_dim(piece_embed, position * width_blk, width_blk, 0)
            fitted_part = lax.dynamic_slice_in_dim(piece_fitted, position * width_blk, width_blk, 0)
            kernel = kernel_block(row_embed, row_square, embed_part).astype(jnp.bfloat16)
            return running + jnp.dot(kernel, fitted_part, preferred_element_type=jnp.float32)

        return lax.fori_loop(0, extent // width_blk, fit_advance, summed)

    return fit_fold


def make_grad(row_embed, row_square, row_wide, adjoint):

    def grad_fold(carry, pieces, offset):
        piece_embed, piece_fitted = pieces
        extent = piece_embed.shape[0]
        width_blk = block_width()

        def grad_advance(position, running):
            row_part, col_part = running
            embed_part = lax.dynamic_slice_in_dim(piece_embed, position * width_blk, width_blk, 0)
            fitted_part = lax.dynamic_slice_in_dim(piece_fitted, position * width_blk, width_blk, 0)
            kernel = kernel_block(row_embed, row_square, embed_part)
            link = lax.dot_general(
                adjoint, fitted_part, (((1,), (1,)), ((), ())), preferred_element_type=jnp.float32
            )
            weight = (link * kernel).astype(jnp.bfloat16)
            across = (
                jnp.dot(weight, embed_part, preferred_element_type=jnp.float32)
                - row_wide * jnp.sum(weight, axis=1, dtype=jnp.float32)[:, None]
            )
            down = lax.dot_general(
                weight, row_embed, (((0,), (0,)), ((), ())), preferred_element_type=jnp.float32
            )
            down = (
                down
                - embed_part.astype(jnp.float32)
                * jnp.sum(weight, axis=0, dtype=jnp.float32)[:, None]
            )
            first_row = offset + position * width_blk
            col_part = lax.dynamic_update_slice_in_dim(col_part, down, first_row, 0)
            return (row_part + across, col_part)

        return lax.fori_loop(0, extent // width_blk, grad_advance, carry)

    return grad_fold


def tiled_plan(curve_embed, solution, targets, lengths, slot_curve, epoch_kernel):
    own_rows = curve_embed.shape[0]
    width = curve_embed.shape[1]
    epochs_count = solution.shape[1]
    group_size = own_rows * lax.axis_size("col")
    column_size = own_rows * lax.axis_size("row")
    fitted_own = jnp.dot(
        solution, epoch_kernel, precision=lax.Precision.HIGHEST, preferred_element_type=jnp.float32
    ).astype(jnp.bfloat16)
    row_embed, row_curve = (
        lax.all_gather(curve_embed, "col", axis=0, tiled=True),
        lax.all_gather(slot_curve, "col", axis=0, tiled=True),
    )
    row_wide = row_embed.astype(jnp.float32)
    row_square = jnp.sum(row_wide * row_wide, axis=1)
    fit_fold = make_fit(row_embed, row_square)
    start_fit = jnp.zeros((group_size, epochs_count), jnp.float32)
    col_embed, col_fitted = (
        lax.all_gather(curve_embed, "row", axis=0, tiled=True),
        lax.all_gather(fitted_own, "row", axis=0, tiled=True),
    )
    fitted_sum = fit_fold(start_fit, (col_embed, col_fitted), 0)
    epochs = jnp.arange(epochs_count, dtype=jnp.int32)
    fitted_mine = lax.psum_scatter(fitted_sum, "col", scatter_dimension=0, tiled=True)
    observed = epochs[None, :] < lengths[:, None]
    adjoint_own = jnp.where(observed, targets.astype(jnp.float32) - fitted_mine, 0.0).astype(
        jnp.bfloat16
    )
    adjoint = lax.all_gather(adjoint_own, "col", axis=0, tiled=True)
    grad_fold = make_grad(row_embed, row_square, row_wide, adjoint)
    start_grad = (
        jnp.zeros((group_size, width), jnp.float32),
        jnp.zeros((column_size, width), jnp.float32),
    )
    row_sum, col_sum = grad_fold(start_grad, (col_embed, col_fitted), 0)
    group_base = lax.axis_index("row") * group_size
    local_curve = (row_curve - group_base).astype(jnp.int32)
    inverse = (
        jnp.zeros((group_size,), jnp.int32)
        .at[local_curve]
        .set(jnp.arange(group_size, dtype=jnp.int32))
    )
    reordered = jnp.take(row_sum, inverse, axis=0)
    factor = 2.0 / width
    row_grad = lax.psum_scatter(reordered, "col", scatter_dimension=0, tiled=True) * factor
    col_grad = lax.psum_scatter(col_sum, "row", scatter_dimension=0, tiled=True) * factor
    return (row_grad, col_grad)


def power_of_two(number):
    return number >= 2 and number & (number - 1) == 0


def per_device(curve_embed, solution, *rest):
    own, width = curve_embed.shape
    rows_axis, cols_axis = lax.axis_size("row"), lax.axis_size("col")
    gathered = own * rows_axis * cols_axis * (width + solution.shape[1]) * 2
    if gathered <= GATHER_LIMIT and rows_axis >= 8 and power_of_two(rows_axis) and cols_axis == 4:
        return gathered_plan(curve_embed, solution, *rest)
    return tiled_plan(curve_embed, solution, *rest)


def solution(mesh):
    in_specs = (
        P(("row", "col"), None),
        P(("row", "col"), None),
        P(("row", "col"), None),
        P(("row", "col")),
        P(("row", "col")),
        P(),
    )
    out_specs = (P(("row", "col"), None), P(("row", "col"), None))
    return jax.shard_map(
        per_device, mesh=mesh, in_specs=in_specs, out_specs=out_specs, check_vma=False
    )
```

```python
import functools
import math

import jax
import jax.numpy as jnp
from jax import lax
from jax.experimental import pallas as pl
from jax.experimental.pallas import tpu as pltpu
from jax.sharding import PartitionSpec as P

GATHER_LIMIT = 4 << 20
DIGIT = 256
BF16, F32 = jnp.bfloat16, jnp.float32
VMEM = pl.BlockSpec(memory_space=pltpu.VMEM)
SMEM = pl.BlockSpec(memory_space=pltpu.SMEM)
PARAMS = pltpu.CompilerParams(vmem_limit_bytes=24 << 20)


def nt_dot(left, right):
    return lax.dot_general(left, right, (((1,), (1,)), ((), ())), preferred_element_type=F32)


def nn_dot(left, right):
    return jnp.dot(left, right, preferred_element_type=F32)


def extended(embed):
    rows, width = embed.shape
    wide = embed.astype(F32)
    square = wide * wide
    high = square.astype(BF16)
    low = (square - high.astype(F32)).astype(BF16)
    ones = jnp.ones((2 * width, width), BF16)
    half = -0.5 * nn_dot(jnp.concatenate([high, low], axis=1), ones)
    first = half.astype(BF16).astype(F32)
    second = (half - first).astype(BF16).astype(F32)
    third = half - first - second
    lane = lax.broadcasted_iota(jnp.int32, (rows, width), 1)

    def lanes(at, one_at):
        tail = jnp.where((lane >= one_at) & (lane < one_at + 3), 1.0, 0.0)
        for offset, term in enumerate((first, second, third)):
            tail = jnp.where(lane == at + offset, term, tail)
        return jnp.concatenate([embed, tail.astype(BF16)], axis=1)

    return lanes


def fetch(sources, held, semaphores):
    copies = [
        pltpu.make_async_copy(source, target, semaphores.at[index])
        for index, (source, target) in enumerate(zip(sources, held))
    ]
    for copy in copies:
        copy.start()
    for copy in copies:
        copy.wait()


def head_kernel(width, *refs):
    sources, columns_ref, held, semaphores = refs[:3], refs[3], refs[4:7], refs[7]
    fetch(sources, held, semaphores)
    embed_ref, solution_ref, epoch_ref = held
    fitted = jnp.dot(
        solution_ref[...], epoch_ref[...], precision=lax.Precision.HIGHEST, preferred_element_type=F32
    )
    columns_ref[...] = jnp.concatenate([embed_ref[...], fitted.astype(BF16)], axis=1)


def targets_kernel(*refs):
    sources, (observed_ref, digits_ref) = refs[:3], refs[4:6]
    held, semaphores = refs[6:9], refs[9]
    fetch(sources, held, semaphores)
    targets_ref, lengths_ref, ids_ref = held
    rows, epochs = targets_ref.shape
    row = lax.broadcasted_iota(jnp.int32, (rows, rows), 0)
    column = lax.broadcasted_iota(jnp.int32, (rows, rows), 1)
    lengths = jnp.sum(
        jnp.where(row == column, lengths_ref[...], 0).astype(F32), axis=1, keepdims=True
    )
    epoch = lax.broadcasted_iota(jnp.int32, (rows, epochs), 1).astype(F32)
    targets = jnp.where(epoch < lengths, targets_ref[...].astype(F32), jnp.inf)
    observed_ref[...] = targets.astype(BF16)
    ids = ids_ref[...]
    place = lax.broadcasted_iota(jnp.int32, (digits_ref.shape[0], rows), 0)
    digits = jnp.where(place == 0, ids // DIGIT, jnp.where(place == 1, ids % DIGIT, 0))
    digits_ref[...] = jnp.zeros(digits_ref.shape, BF16)
    digits_ref[:, :rows] = digits.astype(F32).astype(BF16)


def with_ones(embed):
    return jnp.concatenate([embed, jnp.ones_like(embed)], axis=1)


def gradient(factor, summed, embed):
    width = embed.shape[1]
    return factor * (summed[:, :width] - embed.astype(F32) * summed[:, width:])


def stacked(refs, rows):
    return jnp.concatenate([ref[:rows, :] for ref in refs], axis=0)


def slot_runs(ref, own):
    half = ref.shape[0] // 2
    return jnp.concatenate([ref[:own, :], ref[half : half + own, :]], axis=0)


def joint(refs):
    return jnp.concatenate([ref[...] for ref in refs], axis=0)


def fit_part(scale, own, groups, left_ref, slots_ref, total):
    width = left_ref.shape[1] // 2
    left = left_ref[...]
    slots_left = slot_runs(left_ref, own)
    place = 0
    for group in groups:
        columns = joint(group)
        right = extended(columns[:, :width])(0, 3)
        kernel = jnp.exp2(nt_dot(left, right) * scale).astype(BF16)
        part = nn_dot(kernel, columns[:, width:])
        total = part if total is None else total + part
        slots_ref[:, place : place + columns.shape[0]] = jnp.exp2(
            nt_dot(slots_left, right) * scale
        )
        place += columns.shape[0]
    return total


def pick_kernels(scale, own, first_ref, second_ref, left_ref, picks_ref):
    width = left_ref.shape[1] // 2
    right = extended(stacked((first_ref, second_ref), own)[:, :width])(0, 3)
    picks_ref[...] = jnp.exp2(nt_dot(right, left_ref[...]) * scale)


def main_kernel(scale, own, *refs):
    groups = [(ref,) for ref in refs[:6]]
    left_ref, fit_ref, slots_ref, near_picks_ref, far_picks_ref = refs[6:]
    block, width = left_ref.shape[0] // 2, left_ref.shape[1] // 2
    for part, group in enumerate((groups[0], groups[2])):
        left_ref[part * block : (part + 1) * block, :] = extended(joint(group)[:, :width])(3, 0)
    fit_ref[...] = fit_part(scale, own, groups, left_ref, slots_ref, None)
    pick_kernels(scale, own, refs[0], refs[1], left_ref, near_picks_ref)
    pick_kernels(scale, own, refs[3], refs[4], left_ref, far_picks_ref)


def across_kernel(scale, own, *refs):
    group, (left_ref, before_ref, fit_ref, slots_ref) = refs[:1], refs[1:]
    fit_ref[...] = fit_part(scale, own, (group,), left_ref, slots_ref, before_ref[...])


def column_part(factor, own, adjoint, embed, refs, kernel_ref):
    width = embed.shape[1]
    columns = stacked(refs, own)
    weight = (nt_dot(columns[:, width:], adjoint) * kernel_ref[...]).astype(BF16)
    return gradient(factor, nn_dot(weight, with_ones(embed)), columns[:, :width])


def adjoint_kernel(scale, factor, own, *refs):
    group, (left_ref, before_ref, own_ref, x_ref, picks_ref) = refs[:1], refs[1:6]
    targets_refs, (slots_ref, adjoint_ref, col_ref) = refs[6:8], refs[8:]
    width = left_ref.shape[1] // 2
    fit = fit_part(scale, own, (group,), left_ref, slots_ref, before_ref[...])
    block, run = fit.shape[0] // 2, targets_refs[0].shape[0]
    for at in range(0, fit.shape[0], own):
        part, piece = divmod(at // own, block // own)
        which, first = divmod((2 * piece + part) * own, run)
        values = targets_refs[which][first : first + own, :].astype(F32)
        adjoint = jnp.where(values == jnp.inf, 0.0, values - fit[at : at + own])
        adjoint_ref[at : at + own, :] = adjoint.astype(BF16)
    col_ref[...] = column_part(
        factor, own, adjoint_ref[...], left_ref[:, :width], (own_ref, x_ref), picks_ref
    )


def last_kernel(factor, own, *refs):
    groups = [refs[at : at + 1] for at in range(8)]
    slots_refs, (left_ref, adjoint_ref, picks_ref) = refs[8:11], refs[11:14]
    ids_refs, (col_ref, row_ref) = refs[14:16], refs[16:]
    width = left_ref.shape[1] // 2
    col_ref[...] = column_part(
        factor, own, adjoint_ref[...], left_ref[:, :width], refs[:2], picks_ref
    )
    slots_embed = slot_runs(left_ref, own)[:, :width]
    slots_adjoint = slot_runs(adjoint_ref, own)
    block = left_ref.shape[0] // 2
    places = [(ref, at) for ref in slots_refs for at in range(0, ref.shape[1], block)]
    summed = None
    for group, (kernel_ref, at) in zip(groups, places):
        columns = joint(group)
        link = nt_dot(slots_adjoint, columns[:, width:])
        weight = (link * kernel_ref[:, at : at + block]).astype(BF16)
        part = nn_dot(weight, with_ones(columns[:, :width]))
        summed = part if summed is None else summed + part
    slot_rows = gradient(factor, summed, slots_embed)
    ids = []
    for ref in ids_refs:
        digits = ref[ref.shape[0] - 16 :, :own].astype(F32)
        values = (digits[0:1] * DIGIT + digits[1:2]).astype(jnp.int32)
        ids.append(jnp.broadcast_to(values, (own, own)))
    ids = jnp.concatenate(ids, axis=1)
    wanted = lax.broadcasted_iota(jnp.int32, ids.shape, 0)
    first = lax.axis_index("row") * lax.axis_size("col")
    for mask in (0, 1):
        base = (first + (lax.axis_index("col") ^ mask)) * own
        chosen = (ids == wanted + base).astype(F32)
        row_ref[mask * own : (mask + 1) * own, :] = jnp.dot(
            chosen, slot_rows, precision=lax.Precision.HIGHEST, preferred_element_type=F32
        )


def swap(array, axis, mask):
    pairs = [(index, index ^ mask) for index in range(lax.axis_size(axis))]
    return lax.ppermute(array, axis, pairs)


def joined(array, axis, mask):
    return jnp.concatenate([array, swap(array, axis, mask)], axis=0)


def gathered_plan(curve_embed, solution, targets, lengths, slot_curve, epoch_kernel):
    own, width = curve_embed.shape
    epochs = solution.shape[1]
    rows_axis, cols_axis = lax.axis_size("row"), lax.axis_size("col")
    scale = 2.0 * math.log2(math.e) / width
    factor = 2.0 / width
    shape = jax.ShapeDtypeStruct

    hbm = pl.BlockSpec(memory_space=pltpu.HBM)

    def scratch(arrays):
        buffers = [pltpu.VMEM(array.shape, array.dtype) for array in arrays]
        return [*buffers, pltpu.SemaphoreType.DMA((len(arrays),))]

    arrays = (curve_embed, solution, epoch_kernel)
    columns = pl.pallas_call(
        functools.partial(head_kernel, width),
        out_shape=shape((own, width + epochs), BF16),
        in_specs=[hbm] * 3,
        out_specs=VMEM,
        scratch_shapes=scratch(arrays),
    )(*arrays)
    arrays = (targets, lengths.reshape(1, own), slot_curve.reshape(1, own))
    observed, digits = pl.pallas_call(
        targets_kernel,
        out_shape=(
            shape((own, epochs), BF16),
            shape((16, epochs), BF16),
        ),
        in_specs=[hbm] * 4,
        out_specs=[VMEM] * 2,
        scratch_shapes=scratch(arrays),
        cost_estimate=pl.CostEstimate(flops=1 << 30, bytes_accessed=1 << 16, transcendentals=0),
    )(*arrays, columns)
    step = rows_axis // 2
    labelled = jnp.concatenate([observed, digits], axis=0)
    received, _ = lax.optimization_barrier((swap(columns, "row", step), observed))
    columns = jnp.concatenate([columns, received], axis=0)
    labelled_y = swap(labelled, "col", 2)
    observed = jnp.concatenate([observed, labelled_y[:own]], axis=0)
    while step > 2:
        observed = joined(observed, "row", step)
        step //= 2
        columns = joined(columns, "row", step)
    x_block, y_block = swap(columns, "col", 1), swap(columns, "col", 2)
    across = swap(x_block, "col", 2)
    near = (columns, x_block, y_block)
    far = tuple(swap(array, "row", 1) for array in near)
    block, held = columns.shape[0], 2 * columns.shape[0]

    def call(body, outs, *inputs):
        return pl.pallas_call(
            functools.partial(body, scale, own),
            out_shape=outs,
            in_specs=[VMEM] * len(inputs),
            out_specs=[VMEM] * len(outs),
            compiler_params=PARAMS,
            cost_estimate=pl.CostEstimate(flops=1 << 16, bytes_accessed=1 << 10, transcendentals=0),
        )(*inputs)

    fit_shape, picks_shape = shape((held, epochs), F32), shape((2 * own, held), F32)
    slots = [shape((2 * own, count * block), F32) for count in (6, 1)]
    observed_z = swap(observed, "row", 2)
    left, fit, slots_main, picks_near, picks_far = call(
        main_kernel,
        (shape((held, 2 * width), BF16), fit_shape, slots[0], picks_shape, picks_shape),
        *(*near, *far),
    )
    across, fit, observed_z = lax.optimization_barrier((across, fit, observed_z))
    far_across = swap(across, "row", 1)
    fit, slots_across = call(across_kernel, (fit_shape, slots[1]), across, left, fit)
    slots_last, adjoint, col_far = pl.pallas_call(
        functools.partial(adjoint_kernel, scale, factor, own),
        out_shape=(slots[1], shape((held, epochs), BF16), shape((2 * own, width), F32)),
        in_specs=[VMEM] * 8,
        out_specs=[VMEM] * 3,
        compiler_params=PARAMS,
    )(far_across, left, fit, *far[:2], picks_far, observed, observed_z)
    col_other = swap(col_far, "row", 1)
    col_near, row_part = pl.pallas_call(
        functools.partial(last_kernel, factor, own),
        out_shape=(shape((2 * own, width), F32),) * 2,
        in_specs=[VMEM] * 16,
        out_specs=[VMEM] * 2,
        compiler_params=PARAMS,
        cost_estimate=pl.CostEstimate(flops=1 << 29, bytes_accessed=1 << 20, transcendentals=0),
    )(
        *(*near, *far, across, far_across),
        *(slots_main, slots_across, slots_last),
        *(left, adjoint, picks_near, digits, labelled_y),
    )
    col_part = col_near + col_other
    other = swap(jnp.concatenate([col_part[own:], row_part[own:]], axis=0), "col", 1)
    return row_part[:own] + other[own:], col_part[:own] + other[:own]


def kernel_block(row_embed, row_square, piece_embed):
    piece_wide = piece_embed.astype(jnp.float32)
    products = lax.dot_general(
        row_embed, piece_embed, (((1,), (1,)), ((), ())), preferred_element_type=jnp.float32
    )
    distance = (
        row_square[:, None] + jnp.sum(piece_wide * piece_wide, axis=1)[None, :] - 2.0 * products
    )
    return jnp.exp(-distance / row_embed.shape[1])


def block_width():
    return 256


def make_fit(row_embed, row_square):

    def fit_fold(summed, pieces, offset):
        piece_embed, piece_fitted = pieces
        extent = piece_embed.shape[0]
        width_blk = block_width()

        def fit_advance(position, running):
            embed_part = lax.dynamic_slice_in_dim(piece_embed, position * width_blk, width_blk, 0)
            fitted_part = lax.dynamic_slice_in_dim(piece_fitted, position * width_blk, width_blk, 0)
            kernel = kernel_block(row_embed, row_square, embed_part).astype(jnp.bfloat16)
            return running + jnp.dot(kernel, fitted_part, preferred_element_type=jnp.float32)

        return lax.fori_loop(0, extent // width_blk, fit_advance, summed)

    return fit_fold


def make_grad(row_embed, row_square, row_wide, adjoint):

    def grad_fold(carry, pieces, offset):
        piece_embed, piece_fitted = pieces
        extent = piece_embed.shape[0]
        width_blk = block_width()

        def grad_advance(position, running):
            row_part, col_part = running
            embed_part = lax.dynamic_slice_in_dim(piece_embed, position * width_blk, width_blk, 0)
            fitted_part = lax.dynamic_slice_in_dim(piece_fitted, position * width_blk, width_blk, 0)
            kernel = kernel_block(row_embed, row_square, embed_part)
            link = lax.dot_general(
                adjoint, fitted_part, (((1,), (1,)), ((), ())), preferred_element_type=jnp.float32
            )
            weight = (link * kernel).astype(jnp.bfloat16)
            across = (
                jnp.dot(weight, embed_part, preferred_element_type=jnp.float32)
                - row_wide * jnp.sum(weight, axis=1, dtype=jnp.float32)[:, None]
            )
            down = lax.dot_general(
                weight, row_embed, (((0,), (0,)), ((), ())), preferred_element_type=jnp.float32
            )
            down = (
                down
                - embed_part.astype(jnp.float32)
                * jnp.sum(weight, axis=0, dtype=jnp.float32)[:, None]
            )
            first_row = offset + position * width_blk
            col_part = lax.dynamic_update_slice_in_dim(col_part, down, first_row, 0)
            return (row_part + across, col_part)

        return lax.fori_loop(0, extent // width_blk, grad_advance, carry)

    return grad_fold


def tiled_plan(curve_embed, solution, targets, lengths, slot_curve, epoch_kernel):
    own_rows = curve_embed.shape[0]
    width = curve_embed.shape[1]
    epochs_count = solution.shape[1]
    group_size = own_rows * lax.axis_size("col")
    column_size = own_rows * lax.axis_size("row")
    fitted_own = jnp.dot(
        solution, epoch_kernel, precision=lax.Precision.HIGHEST, preferred_element_type=jnp.float32
    ).astype(jnp.bfloat16)
    row_embed, row_curve = (
        lax.all_gather(curve_embed, "col", axis=0, tiled=True),
        lax.all_gather(slot_curve, "col", axis=0, tiled=True),
    )
    row_wide = row_embed.astype(jnp.float32)
    row_square = jnp.sum(row_wide * row_wide, axis=1)
    fit_fold = make_fit(row_embed, row_square)
    start_fit = jnp.zeros((group_size, epochs_count), jnp.float32)
    col_embed, col_fitted = (
        lax.all_gather(curve_embed, "row", axis=0, tiled=True),
        lax.all_gather(fitted_own, "row", axis=0, tiled=True),
    )
    fitted_sum = fit_fold(start_fit, (col_embed, col_fitted), 0)
    epochs = jnp.arange(epochs_count, dtype=jnp.int32)
    fitted_mine = lax.psum_scatter(fitted_sum, "col", scatter_dimension=0, tiled=True)
    observed = epochs[None, :] < lengths[:, None]
    adjoint_own = jnp.where(observed, targets.astype(jnp.float32) - fitted_mine, 0.0).astype(
        jnp.bfloat16
    )
    adjoint = lax.all_gather(adjoint_own, "col", axis=0, tiled=True)
    grad_fold = make_grad(row_embed, row_square, row_wide, adjoint)
    start_grad = (
        jnp.zeros((group_size, width), jnp.float32),
        jnp.zeros((column_size, width), jnp.float32),
    )
    row_sum, col_sum = grad_fold(start_grad, (col_embed, col_fitted), 0)
    group_base = lax.axis_index("row") * group_size
    local_curve = (row_curve - group_base).astype(jnp.int32)
    inverse = (
        jnp.zeros((group_size,), jnp.int32)
        .at[local_curve]
        .set(jnp.arange(group_size, dtype=jnp.int32))
    )
    reordered = jnp.take(row_sum, inverse, axis=0)
    factor = 2.0 / width
    row_grad = lax.psum_scatter(reordered, "col", scatter_dimension=0, tiled=True) * factor
    col_grad = lax.psum_scatter(col_sum, "row", scatter_dimension=0, tiled=True) * factor
    return (row_grad, col_grad)


def power_of_two(number):
    return number >= 2 and number & (number - 1) == 0


def per_device(curve_embed, solution, *rest):
    own, width = curve_embed.shape
    rows_axis, cols_axis = lax.axis_size("row"), lax.axis_size("col")
    gathered = own * rows_axis * cols_axis * (width + solution.shape[1]) * 2
    if gathered <= GATHER_LIMIT and rows_axis >= 8 and own <= solution.shape[1] and power_of_two(rows_axis) and cols_axis == 4:
        return gathered_plan(curve_embed, solution, *rest)
    return tiled_plan(curve_embed, solution, *rest)


def solution(mesh):
    in_specs = (
        P(("row", "col"), None),
        P(("row", "col"), None),
        P(("row", "col"), None),
        P(("row", "col")),
        P(("row", "col")),
        P(),
    )
    out_specs = (P(("row", "col"), None), P(("row", "col"), None))
    return jax.shard_map(
        per_device, mesh=mesh, in_specs=in_specs, out_specs=out_specs, check_vma=False
    )
```

```python
import functools
import math

import jax
import jax.numpy as jnp
from jax import lax
from jax.experimental import pallas as pl
from jax.experimental.pallas import tpu as pltpu
from jax.sharding import PartitionSpec as P

GATHER_LIMIT = 4 << 20
DIGIT = 256
BF16, F32 = jnp.bfloat16, jnp.float32
VMEM = pl.BlockSpec(memory_space=pltpu.VMEM)
SMEM = pl.BlockSpec(memory_space=pltpu.SMEM)
PARAMS = pltpu.CompilerParams(vmem_limit_bytes=24 << 20)


def nt_dot(left, right):
    return lax.dot_general(left, right, (((1,), (1,)), ((), ())), preferred_element_type=F32)


def nn_dot(left, right):
    return jnp.dot(left, right, preferred_element_type=F32)


def extended(embed):
    rows, width = embed.shape
    wide = embed.astype(F32)
    square = wide * wide
    high = square.astype(BF16)
    low = (square - high.astype(F32)).astype(BF16)
    ones = jnp.ones((2 * width, width), BF16)
    half = -0.5 * nn_dot(jnp.concatenate([high, low], axis=1), ones)
    first = half.astype(BF16).astype(F32)
    second = (half - first).astype(BF16).astype(F32)
    third = half - first - second
    lane = lax.broadcasted_iota(jnp.int32, (rows, width), 1)

    def lanes(at, one_at):
        tail = jnp.where((lane >= one_at) & (lane < one_at + 3), 1.0, 0.0)
        for offset, term in enumerate((first, second, third)):
            tail = jnp.where(lane == at + offset, term, tail)
        return jnp.concatenate([embed, tail.astype(BF16)], axis=1)

    return lanes


def fetch(sources, held, semaphores):
    copies = [
        pltpu.make_async_copy(source, target, semaphores.at[index])
        for index, (source, target) in enumerate(zip(sources, held))
    ]
    for copy in copies:
        copy.start()
    for copy in copies:
        copy.wait()


def head_kernel(width, *refs):
    sources, columns_ref, held, semaphores = refs[:3], refs[3], refs[4:7], refs[7]
    fetch(sources, held, semaphores)
    embed_ref, solution_ref, epoch_ref = held
    fitted = jnp.dot(
        solution_ref[...], epoch_ref[...], precision=lax.Precision.HIGHEST, preferred_element_type=F32
    )
    columns_ref[...] = jnp.concatenate([embed_ref[...], fitted.astype(BF16)], axis=1)


def targets_kernel(*refs):
    sources, (observed_ref, digits_ref) = refs[:3], refs[4:6]
    held, semaphores = refs[6:9], refs[9]
    fetch(sources, held, semaphores)
    targets_ref, lengths_ref, ids_ref = held
    rows, epochs = targets_ref.shape
    row = lax.broadcasted_iota(jnp.int32, (rows, rows), 0)
    column = lax.broadcasted_iota(jnp.int32, (rows, rows), 1)
    lengths = jnp.sum(
        jnp.where(row == column, lengths_ref[...], 0).astype(F32), axis=1, keepdims=True
    )
    epoch = lax.broadcasted_iota(jnp.int32, (rows, epochs), 1).astype(F32)
    targets = jnp.where(epoch < lengths, targets_ref[...].astype(F32), jnp.inf)
    observed_ref[...] = targets.astype(BF16)
    ids = ids_ref[...]
    place = lax.broadcasted_iota(jnp.int32, (digits_ref.shape[0], rows), 0)
    digits = jnp.where(place == 0, ids // DIGIT, jnp.where(place == 1, ids % DIGIT, 0))
    digits_ref[...] = jnp.zeros(digits_ref.shape, BF16)
    digits_ref[:, :rows] = digits.astype(F32).astype(BF16)


def with_ones(embed):
    return jnp.concatenate([embed, jnp.ones_like(embed)], axis=1)


def gradient(factor, summed, embed):
    width = embed.shape[1]
    return factor * (summed[:, :width] - embed.astype(F32) * summed[:, width:])


def stacked(refs, rows):
    return jnp.concatenate([ref[:rows, :] for ref in refs], axis=0)


def slot_runs(ref, own):
    half = ref.shape[0] // 2
    return jnp.concatenate([ref[:own, :], ref[half : half + own, :]], axis=0)


def fit_part(scale, own, columns, rights, left, slots_ref, total):
    width, half, place = left.shape[1] // 2, left.shape[0] // 2, 0
    for values, right in zip(columns, rights):
        kernel = jnp.exp2(nt_dot(left, right) * scale)
        slots_ref[:, place : place + right.shape[0]] = jnp.concatenate(
            [kernel[:own], kernel[half : half + own]], axis=0
        )
        part = nn_dot(kernel.astype(BF16), values[:, width:])
        total = part if total is None else total + part
        place += right.shape[0]
    return total


def main_kernel(scale, own, *refs):
    columns, (left_ref, fit_ref, slots_ref, *picks_refs) = [ref[...] for ref in refs[:6]], refs[6:]
    width = left_ref.shape[1] // 2
    forms = [extended(values[:, :width]) for values in columns]
    left = jnp.concatenate([forms[0](3, 0), forms[2](3, 0)], axis=0)
    left_ref[...] = left
    rights = [form(0, 3) for form in forms]
    fit_ref[...] = fit_part(scale, own, columns, rights, left, slots_ref, None)
    for picks_ref, first in zip(picks_refs, (0, 3)):
        picked = jnp.concatenate([rights[first][:own], rights[first + 1][:own]], axis=0)
        picks_ref[...] = jnp.exp2(nt_dot(picked, left) * scale)


def across_part(scale, own, columns_ref, left_ref, before_ref, slots_ref):
    columns, width = columns_ref[...], left_ref.shape[1] // 2
    right = extended(columns[:, :width])(0, 3)
    return fit_part(scale, own, [columns], [right], left_ref[...], slots_ref, before_ref[...])


def across_kernel(scale, own, columns_ref, left_ref, before_ref, fit_ref, slots_ref):
    fit_ref[...] = across_part(scale, own, columns_ref, left_ref, before_ref, slots_ref)


def column_part(factor, own, adjoint, embed, refs, kernel_ref):
    width = embed.shape[1]
    columns = stacked(refs, own)
    weight = (nt_dot(columns[:, width:], adjoint) * kernel_ref[...]).astype(BF16)
    return gradient(factor, nn_dot(weight, with_ones(embed)), columns[:, :width])


def adjoint_kernel(scale, factor, own, *refs):
    across_ref, left_ref, before_ref, own_ref, x_ref, picks_ref = refs[:6]
    targets_refs, (slots_ref, adjoint_ref, col_ref) = refs[6:8], refs[8:]
    width = left_ref.shape[1] // 2
    fit = across_part(scale, own, across_ref, left_ref, before_ref, slots_ref)
    block, run = fit.shape[0] // 2, targets_refs[0].shape[0]
    for at in range(0, fit.shape[0], own):
        part, piece = divmod(at // own, block // own)
        which, first = divmod((2 * piece + part) * own, run)
        values = targets_refs[which][first : first + own, :].astype(F32)
        adjoint = jnp.where(values == jnp.inf, 0.0, values - fit[at : at + own])
        adjoint_ref[at : at + own, :] = adjoint.astype(BF16)
    col_ref[...] = column_part(
        factor, own, adjoint_ref[...], left_ref[:, :width], (own_ref, x_ref), picks_ref
    )


def last_kernel(factor, own, *refs):
    columns_refs = refs[:8]
    slots_refs, (left_ref, adjoint_ref, picks_ref) = refs[8:11], refs[11:14]
    ids_refs, (col_ref, row_ref) = refs[14:16], refs[16:]
    width = left_ref.shape[1] // 2
    col_ref[...] = column_part(
        factor, own, adjoint_ref[...], left_ref[:, :width], refs[:2], picks_ref
    )
    slots_embed = slot_runs(left_ref, own)[:, :width]
    slots_adjoint = slot_runs(adjoint_ref, own)
    block = left_ref.shape[0] // 2
    places = [(ref, at) for ref in slots_refs for at in range(0, ref.shape[1], block)]
    summed = None
    for columns_ref, (kernel_ref, at) in zip(columns_refs, places):
        columns = columns_ref[...]
        link = nt_dot(slots_adjoint, columns[:, width:])
        weight = (link * kernel_ref[:, at : at + block]).astype(BF16)
        part = nn_dot(weight, with_ones(columns[:, :width]))
        summed = part if summed is None else summed + part
    slot_rows = gradient(factor, summed, slots_embed)
    ids = []
    for ref in ids_refs:
        digits = ref[ref.shape[0] - 16 :, :own].astype(F32)
        values = (digits[0:1] * DIGIT + digits[1:2]).astype(jnp.int32)
        ids.append(jnp.broadcast_to(values, (2 * own, own)))
    ids = jnp.concatenate(ids, axis=1)
    wanted = lax.broadcasted_iota(jnp.int32, ids.shape, 0)
    first = lax.axis_index("row") * lax.axis_size("col")
    bases = [(first + (lax.axis_index("col") ^ mask)) * own for mask in (0, 1)]
    wanted += jnp.where(wanted < own, bases[0], bases[1] - own)
    chosen = jnp.where(ids == wanted, 1.0, 0.0).astype(BF16)
    high = slot_rows.astype(BF16)
    rest = slot_rows - high.astype(F32)
    middle = rest.astype(BF16)
    low = (rest - middle.astype(F32)).astype(BF16)
    terms = nn_dot(chosen, jnp.concatenate([high, middle, low], axis=1))
    row_ref[...] = terms[:, :width] + terms[:, width : 2 * width] + terms[:, 2 * width :]


def swap(array, axis, mask):
    pairs = [(index, index ^ mask) for index in range(lax.axis_size(axis))]
    return lax.ppermute(array, axis, pairs)


def joined(array, axis, mask):
    return jnp.concatenate([array, swap(array, axis, mask)], axis=0)


def gathered_plan(curve_embed, solution, targets, lengths, slot_curve, epoch_kernel):
    own, width = curve_embed.shape
    epochs = solution.shape[1]
    rows_axis, cols_axis = lax.axis_size("row"), lax.axis_size("col")
    scale = 2.0 * math.log2(math.e) / width
    factor = 2.0 / width
    shape = jax.ShapeDtypeStruct

    hbm = pl.BlockSpec(memory_space=pltpu.HBM)

    def scratch(arrays):
        buffers = [pltpu.VMEM(array.shape, array.dtype) for array in arrays]
        return [*buffers, pltpu.SemaphoreType.DMA((len(arrays),))]

    arrays = (curve_embed, solution, epoch_kernel)
    columns = pl.pallas_call(
        functools.partial(head_kernel, width),
        out_shape=shape((own, width + epochs), BF16),
        in_specs=[hbm] * 3,
        out_specs=VMEM,
        scratch_shapes=scratch(arrays),
    )(*arrays)
    arrays = (targets, lengths.reshape(1, own), slot_curve.reshape(1, own))
    observed, digits = pl.pallas_call(
        targets_kernel,
        out_shape=(
            shape((own, epochs), BF16),
            shape((16, epochs), BF16),
        ),
        in_specs=[hbm] * 4,
        out_specs=[VMEM] * 2,
        scratch_shapes=scratch(arrays),
        cost_estimate=pl.CostEstimate(flops=1 << 30, bytes_accessed=1 << 16, transcendentals=0),
    )(*arrays, columns)
    step = rows_axis // 2
    labelled = jnp.concatenate([observed, digits], axis=0)
    received, _ = lax.optimization_barrier((swap(columns, "row", step), observed))
    columns = jnp.concatenate([columns, received], axis=0)
    labelled_y = swap(labelled, "col", 2)
    observed = jnp.concatenate([observed, labelled_y[:own]], axis=0)
    while step > 2:
        observed = joined(observed, "row", step)
        step //= 2
        columns = joined(columns, "row", step)
    x_block, y_block = swap(columns, "col", 1), swap(columns, "col", 2)
    across = swap(x_block, "col", 2)
    near = (columns, x_block, y_block)
    far = tuple(swap(array, "row", 1) for array in near)
    block, held = columns.shape[0], 2 * columns.shape[0]

    def call(body, outs, *inputs):
        return pl.pallas_call(
            functools.partial(body, scale, own),
            out_shape=outs,
            in_specs=[VMEM] * len(inputs),
            out_specs=[VMEM] * len(outs),
            compiler_params=PARAMS,
            cost_estimate=pl.CostEstimate(flops=1 << 16, bytes_accessed=1 << 10, transcendentals=0),
        )(*inputs)

    fit_shape, picks_shape = shape((held, epochs), F32), shape((2 * own, held), F32)
    slots = [shape((2 * own, count * block), F32) for count in (6, 1)]
    observed_z = swap(observed, "row", 2)
    left, fit, slots_main, picks_near, picks_far = call(
        main_kernel,
        (shape((held, 2 * width), BF16), fit_shape, slots[0], picks_shape, picks_shape),
        *(*near, *far),
    )
    across, fit, observed_z = lax.optimization_barrier((across, fit, observed_z))
    far_across = swap(across, "row", 1)
    fit, slots_across = call(across_kernel, (fit_shape, slots[1]), across, left, fit)
    slots_last, adjoint, col_far = pl.pallas_call(
        functools.partial(adjoint_kernel, scale, factor, own),
        out_shape=(slots[1], shape((held, epochs), BF16), shape((2 * own, width), F32)),
        in_specs=[VMEM] * 8,
        out_specs=[VMEM] * 3,
        compiler_params=PARAMS,
    )(far_across, left, fit, *far[:2], picks_far, observed, observed_z)
    col_other = swap(col_far, "row", 1)
    col_near, row_part = pl.pallas_call(
        functools.partial(last_kernel, factor, own),
        out_shape=(shape((2 * own, width), F32),) * 2,
        in_specs=[VMEM] * 16,
        out_specs=[VMEM] * 2,
        compiler_params=PARAMS,
        cost_estimate=pl.CostEstimate(flops=1 << 29, bytes_accessed=1 << 20, transcendentals=0),
    )(
        *(*near, *far, across, far_across),
        *(slots_main, slots_across, slots_last),
        *(left, adjoint, picks_near, digits, labelled_y),
    )
    col_part = col_near + col_other
    other = swap(jnp.concatenate([col_part[own:], row_part[own:]], axis=0), "col", 1)
    return row_part[:own] + other[own:], col_part[:own] + other[:own]


def kernel_block(row_embed, row_square, piece_embed):
    piece_wide = piece_embed.astype(jnp.float32)
    products = lax.dot_general(
        row_embed, piece_embed, (((1,), (1,)), ((), ())), preferred_element_type=jnp.float32
    )
    distance = (
        row_square[:, None] + jnp.sum(piece_wide * piece_wide, axis=1)[None, :] - 2.0 * products
    )
    return jnp.exp(-distance / row_embed.shape[1])


def block_width():
    return 256


def make_fit(row_embed, row_square):

    def fit_fold(summed, pieces, offset):
        piece_embed, piece_fitted = pieces
        extent = piece_embed.shape[0]
        width_blk = block_width()

        def fit_advance(position, running):
            embed_part = lax.dynamic_slice_in_dim(piece_embed, position * width_blk, width_blk, 0)
            fitted_part = lax.dynamic_slice_in_dim(piece_fitted, position * width_blk, width_blk, 0)
            kernel = kernel_block(row_embed, row_square, embed_part).astype(jnp.bfloat16)
            return running + jnp.dot(kernel, fitted_part, preferred_element_type=jnp.float32)

        return lax.fori_loop(0, extent // width_blk, fit_advance, summed)

    return fit_fold


def make_grad(row_embed, row_square, row_wide, adjoint):

    def grad_fold(carry, pieces, offset):
        piece_embed, piece_fitted = pieces
        extent = piece_embed.shape[0]
        width_blk = block_width()

        def grad_advance(position, running):
            row_part, col_part = running
            embed_part = lax.dynamic_slice_in_dim(piece_embed, position * width_blk, width_blk, 0)
            fitted_part = lax.dynamic_slice_in_dim(piece_fitted, position * width_blk, width_blk, 0)
            kernel = kernel_block(row_embed, row_square, embed_part)
            link = lax.dot_general(
                adjoint, fitted_part, (((1,), (1,)), ((), ())), preferred_element_type=jnp.float32
            )
            weight = (link * kernel).astype(jnp.bfloat16)
            across = (
                jnp.dot(weight, embed_part, preferred_element_type=jnp.float32)
                - row_wide * jnp.sum(weight, axis=1, dtype=jnp.float32)[:, None]
            )
            down = lax.dot_general(
                weight, row_embed, (((0,), (0,)), ((), ())), preferred_element_type=jnp.float32
            )
            down = (
                down
                - embed_part.astype(jnp.float32)
                * jnp.sum(weight, axis=0, dtype=jnp.float32)[:, None]
            )
            first_row = offset + position * width_blk
            col_part = lax.dynamic_update_slice_in_dim(col_part, down, first_row, 0)
            return (row_part + across, col_part)

        return lax.fori_loop(0, extent // width_blk, grad_advance, carry)

    return grad_fold


def tiled_plan(curve_embed, solution, targets, lengths, slot_curve, epoch_kernel):
    own_rows = curve_embed.shape[0]
    width = curve_embed.shape[1]
    epochs_count = solution.shape[1]
    group_size = own_rows * lax.axis_size("col")
    column_size = own_rows * lax.axis_size("row")
    fitted_own = jnp.dot(
        solution, epoch_kernel, precision=lax.Precision.HIGHEST, preferred_element_type=jnp.float32
    ).astype(jnp.bfloat16)
    row_embed, row_curve = (
        lax.all_gather(curve_embed, "col", axis=0, tiled=True),
        lax.all_gather(slot_curve, "col", axis=0, tiled=True),
    )
    row_wide = row_embed.astype(jnp.float32)
    row_square = jnp.sum(row_wide * row_wide, axis=1)
    fit_fold = make_fit(row_embed, row_square)
    start_fit = jnp.zeros((group_size, epochs_count), jnp.float32)
    col_embed, col_fitted = (
        lax.all_gather(curve_embed, "row", axis=0, tiled=True),
        lax.all_gather(fitted_own, "row", axis=0, tiled=True),
    )
    fitted_sum = fit_fold(start_fit, (col_embed, col_fitted), 0)
    epochs = jnp.arange(epochs_count, dtype=jnp.int32)
    fitted_mine = lax.psum_scatter(fitted_sum, "col", scatter_dimension=0, tiled=True)
    observed = epochs[None, :] < lengths[:, None]
    adjoint_own = jnp.where(observed, targets.astype(jnp.float32) - fitted_mine, 0.0).astype(
        jnp.bfloat16
    )
    adjoint = lax.all_gather(adjoint_own, "col", axis=0, tiled=True)
    grad_fold = make_grad(row_embed, row_square, row_wide, adjoint)
    start_grad = (
        jnp.zeros((group_size, width), jnp.float32),
        jnp.zeros((column_size, width), jnp.float32),
    )
    row_sum, col_sum = grad_fold(start_grad, (col_embed, col_fitted), 0)
    group_base = lax.axis_index("row") * group_size
    local_curve = (row_curve - group_base).astype(jnp.int32)
    inverse = (
        jnp.zeros((group_size,), jnp.int32)
        .at[local_curve]
        .set(jnp.arange(group_size, dtype=jnp.int32))
    )
    reordered = jnp.take(row_sum, inverse, axis=0)
    factor = 2.0 / width
    row_grad = lax.psum_scatter(reordered, "col", scatter_dimension=0, tiled=True) * factor
    col_grad = lax.psum_scatter(col_sum, "row", scatter_dimension=0, tiled=True) * factor
    return (row_grad, col_grad)


def power_of_two(number):
    return number >= 2 and number & (number - 1) == 0


def per_device(curve_embed, solution, *rest):
    own, width = curve_embed.shape
    rows_axis, cols_axis = lax.axis_size("row"), lax.axis_size("col")
    gathered = own * rows_axis * cols_axis * (width + solution.shape[1]) * 2
    if gathered <= GATHER_LIMIT and rows_axis >= 8 and own <= solution.shape[1] and power_of_two(rows_axis) and cols_axis == 4:
        return gathered_plan(curve_embed, solution, *rest)
    return tiled_plan(curve_embed, solution, *rest)


def solution(mesh):
    in_specs = (
        P(("row", "col"), None),
        P(("row", "col"), None),
        P(("row", "col"), None),
        P(("row", "col")),
        P(("row", "col")),
        P(),
    )
    out_specs = (P(("row", "col"), None), P(("row", "col"), None))
    return jax.shard_map(
        per_device, mesh=mesh, in_specs=in_specs, out_specs=out_specs, check_vma=False
    )
```

```python
import functools
import math

import jax
import jax.numpy as jnp
from jax import lax
from jax.experimental import pallas as pl
from jax.experimental.pallas import tpu as pltpu
from jax.sharding import PartitionSpec as P

GATHER_LIMIT = 4 << 20
DIGIT = 256
BF16, F32 = jnp.bfloat16, jnp.float32
VMEM = pl.BlockSpec(memory_space=pltpu.VMEM)
SMEM = pl.BlockSpec(memory_space=pltpu.SMEM)
PARAMS = pltpu.CompilerParams(vmem_limit_bytes=24 << 20)


def nt_dot(left, right):
    return lax.dot_general(left, right, (((1,), (1,)), ((), ())), preferred_element_type=F32)


def nn_dot(left, right):
    return jnp.dot(left, right, preferred_element_type=F32)


def extended(embed):
    rows, width = embed.shape
    wide = embed.astype(F32)
    square = wide * wide
    high = square.astype(BF16)
    low = (square - high.astype(F32)).astype(BF16)
    ones = jnp.ones((2 * width, width), BF16)
    half = -0.5 * nn_dot(jnp.concatenate([high, low], axis=1), ones)
    first = half.astype(BF16).astype(F32)
    second = (half - first).astype(BF16).astype(F32)
    third = half - first - second
    lane = lax.broadcasted_iota(jnp.int32, (rows, width), 1)

    def lanes(at, one_at):
        tail = jnp.where((lane >= one_at) & (lane < one_at + 3), 1.0, 0.0)
        for offset, term in enumerate((first, second, third)):
            tail = jnp.where(lane == at + offset, term, tail)
        return jnp.concatenate([embed, tail.astype(BF16)], axis=1)

    return lanes


def fetch(sources, held, semaphores):
    copies = [
        pltpu.make_async_copy(source, target, semaphores.at[index])
        for index, (source, target) in enumerate(zip(sources, held))
    ]
    for copy in copies:
        copy.start()
    for copy in copies:
        copy.wait()


def head_kernel(width, *refs):
    sources, columns_ref, held, semaphores = refs[:3], refs[3], refs[4:7], refs[7]
    fetch(sources, held, semaphores)
    embed_ref, solution_ref, epoch_ref = held
    fitted = jnp.dot(
        solution_ref[...], epoch_ref[...], precision=lax.Precision.HIGHEST, preferred_element_type=F32
    )
    columns_ref[...] = jnp.concatenate([embed_ref[...], fitted.astype(BF16)], axis=1)


def targets_kernel(*refs):
    sources, (observed_ref, digits_ref) = refs[:3], refs[4:6]
    held, semaphores = refs[6:9], refs[9]
    fetch(sources, held, semaphores)
    targets_ref, lengths_ref, ids_ref = held
    rows, epochs = targets_ref.shape
    row = lax.broadcasted_iota(jnp.int32, (rows, rows), 0)
    column = lax.broadcasted_iota(jnp.int32, (rows, rows), 1)
    lengths = jnp.sum(
        jnp.where(row == column, lengths_ref[...], 0).astype(F32), axis=1, keepdims=True
    )
    epoch = lax.broadcasted_iota(jnp.int32, (rows, epochs), 1).astype(F32)
    targets = jnp.where(epoch < lengths, targets_ref[...].astype(F32), jnp.inf)
    observed_ref[...] = targets.astype(BF16)
    ids = ids_ref[...]
    place = lax.broadcasted_iota(jnp.int32, (digits_ref.shape[0], rows), 0)
    digits = jnp.where(place == 0, ids // DIGIT, jnp.where(place == 1, ids % DIGIT, 0))
    digits_ref[...] = jnp.zeros(digits_ref.shape, BF16)
    digits_ref[:, :rows] = digits.astype(F32).astype(BF16)


def with_ones(embed):
    return jnp.concatenate([embed, jnp.ones_like(embed)], axis=1)


def gradient(factor, summed, embed):
    width = embed.shape[1]
    return factor * (summed[:, :width] - embed.astype(F32) * summed[:, width:])


def stacked(refs, rows):
    return jnp.concatenate([ref[:rows, :] for ref in refs], axis=0)


def slot_runs(ref, own):
    half = ref.shape[0] // 2
    return jnp.concatenate([ref[:own, :], ref[half : half + own, :]], axis=0)


def fit_part(scale, own, columns, rights, left, slots_ref, total):
    width, half, place = left.shape[1] // 2, left.shape[0] // 2, 0
    for values, right in zip(columns, rights):
        kernel = jnp.exp2(nt_dot(left, right) * scale)
        slots_ref[:, place : place + right.shape[0]] = jnp.concatenate(
            [kernel[:own], kernel[half : half + own]], axis=0
        )
        part = nn_dot(kernel.astype(BF16), values[:, width:])
        total = part if total is None else total + part
        place += right.shape[0]
    return total


def main_kernel(scale, own, *refs):
    columns, (left_ref, fit_ref, slots_ref, *picks_refs) = [ref[...] for ref in refs[:6]], refs[6:]
    width = left_ref.shape[1] // 2
    forms = [extended(values[:, :width]) for values in columns]
    left = jnp.concatenate([forms[0](3, 0), forms[2](3, 0)], axis=0)
    left_ref[...] = left
    rights = [form(0, 3) for form in forms]
    fit_ref[...] = fit_part(scale, own, columns, rights, left, slots_ref, None)
    for picks_ref, first in zip(picks_refs, (0, 3)):
        picked = jnp.concatenate([rights[first][:own], rights[first + 1][:own]], axis=0)
        picks_ref[...] = jnp.exp2(nt_dot(picked, left) * scale)


def across_part(scale, own, columns_ref, left_ref, before_ref, slots_ref):
    columns, width = columns_ref[...], left_ref.shape[1] // 2
    right = extended(columns[:, :width])(0, 3)
    return fit_part(scale, own, [columns], [right], left_ref[...], slots_ref, before_ref[...])


def across_kernel(scale, own, columns_ref, left_ref, before_ref, fit_ref, slots_ref):
    fit_ref[...] = across_part(scale, own, columns_ref, left_ref, before_ref, slots_ref)


def column_part(factor, own, adjoint, embed, refs, kernel_ref):
    width = embed.shape[1]
    columns = stacked(refs, own)
    weight = (nt_dot(columns[:, width:], adjoint) * kernel_ref[...]).astype(BF16)
    return gradient(factor, nn_dot(weight, with_ones(embed)), columns[:, :width])


def adjoint_kernel(scale, factor, own, *refs):
    across_ref, left_ref, before_ref, own_ref, x_ref, picks_ref = refs[:6]
    targets_refs, (slots_ref, adjoint_ref, col_ref) = refs[6:8], refs[8:]
    width = left_ref.shape[1] // 2
    fit = across_part(scale, own, across_ref, left_ref, before_ref, slots_ref)
    block, run = fit.shape[0] // 2, targets_refs[0].shape[0]
    for at in range(0, fit.shape[0], own):
        part, piece = divmod(at // own, block // own)
        which, first = divmod((2 * piece + part) * own, run)
        values = targets_refs[which][first : first + own, :].astype(F32)
        adjoint = jnp.where(values == jnp.inf, 0.0, values - fit[at : at + own])
        adjoint_ref[at : at + own, :] = adjoint.astype(BF16)
    col_ref[...] = column_part(
        factor, own, adjoint_ref[...], left_ref[:, :width], (own_ref, x_ref), picks_ref
    )


def last_kernel(factor, own, *refs):
    columns_refs = refs[:8]
    slots_refs, (left_ref, adjoint_ref, picks_ref) = refs[8:11], refs[11:14]
    ids_refs, (col_ref, row_ref) = refs[14:16], refs[16:]
    width = left_ref.shape[1] // 2
    col_ref[...] = column_part(
        factor, own, adjoint_ref[...], left_ref[:, :width], refs[:2], picks_ref
    )
    slots_embed = slot_runs(left_ref, own)[:, :width]
    slots_adjoint = slot_runs(adjoint_ref, own)
    block = left_ref.shape[0] // 2
    places = [(ref, at) for ref in slots_refs for at in range(0, ref.shape[1], block)]
    summed = None
    for columns_ref, (kernel_ref, at) in zip(columns_refs, places):
        columns = columns_ref[...]
        link = nt_dot(slots_adjoint, columns[:, width:])
        weight = (link * kernel_ref[:, at : at + block]).astype(BF16)
        part = nn_dot(weight, with_ones(columns[:, :width]))
        summed = part if summed is None else summed + part
    slot_rows = gradient(factor, summed, slots_embed)
    ids = []
    for ref in ids_refs:
        digits = ref[ref.shape[0] - 16 :, :own].astype(F32)
        values = (digits[0:1] * DIGIT + digits[1:2]).astype(jnp.int32)
        ids.append(jnp.broadcast_to(values, (2 * own, own)))
    ids = jnp.concatenate(ids, axis=1)
    wanted = lax.broadcasted_iota(jnp.int32, ids.shape, 0)
    first = lax.axis_index("row") * lax.axis_size("col")
    bases = [(first + (lax.axis_index("col") ^ mask)) * own for mask in (0, 1)]
    wanted += jnp.where(wanted < own, bases[0], bases[1] - own)
    chosen = jnp.where(ids == wanted, 1.0, 0.0).astype(BF16)
    high = slot_rows.astype(BF16)
    rest = slot_rows - high.astype(F32)
    middle = rest.astype(BF16)
    low = (rest - middle.astype(F32)).astype(BF16)
    terms = nn_dot(chosen, jnp.concatenate([high, middle, low], axis=1))
    row_ref[...] = terms[:, :width] + terms[:, width : 2 * width] + terms[:, 2 * width :]


def swap(array, axis, mask):
    pairs = [(index, index ^ mask) for index in range(lax.axis_size(axis))]
    return lax.ppermute(array, axis, pairs)


def joined(array, axis, mask):
    return jnp.concatenate([array, swap(array, axis, mask)], axis=0)


def gathered_plan(curve_embed, solution, targets, lengths, slot_curve, epoch_kernel):
    own, width = curve_embed.shape
    epochs = solution.shape[1]
    rows_axis, cols_axis = lax.axis_size("row"), lax.axis_size("col")
    scale = 2.0 * math.log2(math.e) / width
    factor = 2.0 / width
    shape = jax.ShapeDtypeStruct

    hbm = pl.BlockSpec(memory_space=pltpu.HBM)

    def scratch(arrays):
        buffers = [pltpu.VMEM(array.shape, array.dtype) for array in arrays]
        return [*buffers, pltpu.SemaphoreType.DMA((len(arrays),))]

    arrays = (curve_embed, solution, epoch_kernel)
    columns = pl.pallas_call(
        functools.partial(head_kernel, width),
        out_shape=shape((own, width + epochs), BF16),
        in_specs=[hbm] * 3,
        out_specs=VMEM,
        scratch_shapes=scratch(arrays),
    )(*arrays)
    arrays = (targets, lengths.reshape(1, own), slot_curve.reshape(1, own))
    observed, digits = pl.pallas_call(
        targets_kernel,
        out_shape=(
            shape((own, epochs), BF16),
            shape((16, epochs), BF16),
        ),
        in_specs=[hbm] * 4,
        out_specs=[VMEM] * 2,
        scratch_shapes=scratch(arrays),
        cost_estimate=pl.CostEstimate(flops=1 << 30, bytes_accessed=1 << 16, transcendentals=0),
    )(*arrays, columns)
    step = rows_axis // 2
    labelled = jnp.concatenate([observed, digits], axis=0)
    received, _ = lax.optimization_barrier((swap(columns, "row", step), observed))
    columns = jnp.concatenate([columns, received], axis=0)
    labelled_y = swap(labelled, "col", 2)
    observed = jnp.concatenate([observed, labelled_y[:own]], axis=0)
    while step > 2:
        observed = joined(observed, "row", step)
        step //= 2
        columns = joined(columns, "row", step)
    x_block, y_block = swap(columns, "col", 1), swap(columns, "col", 2)
    across = swap(x_block, "col", 2)
    near = (columns, x_block, y_block)
    far = tuple(swap(array, "row", 1) for array in near)
    block, held = columns.shape[0], 2 * columns.shape[0]

    def call(body, outs, *inputs):
        return pl.pallas_call(
            functools.partial(body, scale, own),
            out_shape=outs,
            in_specs=[VMEM] * len(inputs),
            out_specs=[VMEM] * len(outs),
            compiler_params=PARAMS,
            cost_estimate=pl.CostEstimate(flops=1 << 16, bytes_accessed=1 << 10, transcendentals=0),
        )(*inputs)

    fit_shape, picks_shape = shape((held, epochs), F32), shape((2 * own, held), F32)
    slots = [shape((2 * own, count * block), F32) for count in (6, 1)]
    observed_z = swap(observed, "row", 2)
    left, fit, slots_main, picks_near, picks_far = call(
        main_kernel,
        (shape((held, 2 * width), BF16), fit_shape, slots[0], picks_shape, picks_shape),
        *(*near, *far),
    )
    sent, _, observed_z = lax.optimization_barrier((across, fit, observed_z))
    far_across = swap(sent, "row", 1)
    fit, slots_across = call(across_kernel, (fit_shape, slots[1]), across, left, fit)
    slots_last, adjoint, col_far = pl.pallas_call(
        functools.partial(adjoint_kernel, scale, factor, own),
        out_shape=(slots[1], shape((held, epochs), BF16), shape((2 * own, width), F32)),
        in_specs=[VMEM] * 8,
        out_specs=[VMEM] * 3,
        compiler_params=PARAMS,
    )(far_across, left, fit, *far[:2], picks_far, observed, observed_z)
    col_other = swap(col_far, "row", 1)
    col_near, row_part = pl.pallas_call(
        functools.partial(last_kernel, factor, own),
        out_shape=(shape((2 * own, width), F32),) * 2,
        in_specs=[VMEM] * 16,
        out_specs=[VMEM] * 2,
        compiler_params=PARAMS,
        cost_estimate=pl.CostEstimate(flops=1 << 29, bytes_accessed=1 << 20, transcendentals=0),
    )(
        *(*near, *far, across, far_across),
        *(slots_main, slots_across, slots_last),
        *(left, adjoint, picks_near, digits, labelled_y),
    )
    col_part = col_near + col_other
    other = swap(jnp.concatenate([col_part[own:], row_part[own:]], axis=0), "col", 1)
    return row_part[:own] + other[own:], col_part[:own] + other[:own]


def kernel_block(row_embed, row_square, piece_embed):
    piece_wide = piece_embed.astype(jnp.float32)
    products = lax.dot_general(
        row_embed, piece_embed, (((1,), (1,)), ((), ())), preferred_element_type=jnp.float32
    )
    distance = (
        row_square[:, None] + jnp.sum(piece_wide * piece_wide, axis=1)[None, :] - 2.0 * products
    )
    return jnp.exp(-distance / row_embed.shape[1])


def block_width():
    return 256


def make_fit(row_embed, row_square):

    def fit_fold(summed, pieces, offset):
        piece_embed, piece_fitted = pieces
        extent = piece_embed.shape[0]
        width_blk = block_width()

        def fit_advance(position, running):
            embed_part = lax.dynamic_slice_in_dim(piece_embed, position * width_blk, width_blk, 0)
            fitted_part = lax.dynamic_slice_in_dim(piece_fitted, position * width_blk, width_blk, 0)
            kernel = kernel_block(row_embed, row_square, embed_part).astype(jnp.bfloat16)
            return running + jnp.dot(kernel, fitted_part, preferred_element_type=jnp.float32)

        return lax.fori_loop(0, extent // width_blk, fit_advance, summed)

    return fit_fold


def make_grad(row_embed, row_square, row_wide, adjoint):

    def grad_fold(carry, pieces, offset):
        piece_embed, piece_fitted = pieces
        extent = piece_embed.shape[0]
        width_blk = block_width()

        def grad_advance(position, running):
            row_part, col_part = running
            embed_part = lax.dynamic_slice_in_dim(piece_embed, position * width_blk, width_blk, 0)
            fitted_part = lax.dynamic_slice_in_dim(piece_fitted, position * width_blk, width_blk, 0)
            kernel = kernel_block(row_embed, row_square, embed_part)
            link = lax.dot_general(
                adjoint, fitted_part, (((1,), (1,)), ((), ())), preferred_element_type=jnp.float32
            )
            weight = (link * kernel).astype(jnp.bfloat16)
            across = (
                jnp.dot(weight, embed_part, preferred_element_type=jnp.float32)
                - row_wide * jnp.sum(weight, axis=1, dtype=jnp.float32)[:, None]
            )
            down = lax.dot_general(
                weight, row_embed, (((0,), (0,)), ((), ())), preferred_element_type=jnp.float32
            )
            down = (
                down
                - embed_part.astype(jnp.float32)
                * jnp.sum(weight, axis=0, dtype=jnp.float32)[:, None]
            )
            first_row = offset + position * width_blk
            col_part = lax.dynamic_update_slice_in_dim(col_part, down, first_row, 0)
            return (row_part + across, col_part)

        return lax.fori_loop(0, extent // width_blk, grad_advance, carry)

    return grad_fold


def tiled_plan(curve_embed, solution, targets, lengths, slot_curve, epoch_kernel):
    own_rows = curve_embed.shape[0]
    width = curve_embed.shape[1]
    epochs_count = solution.shape[1]
    group_size = own_rows * lax.axis_size("col")
    column_size = own_rows * lax.axis_size("row")
    fitted_own = jnp.dot(
        solution, epoch_kernel, precision=lax.Precision.HIGHEST, preferred_element_type=jnp.float32
    ).astype(jnp.bfloat16)
    row_embed, row_curve = (
        lax.all_gather(curve_embed, "col", axis=0, tiled=True),
        lax.all_gather(slot_curve, "col", axis=0, tiled=True),
    )
    row_wide = row_embed.astype(jnp.float32)
    row_square = jnp.sum(row_wide * row_wide, axis=1)
    fit_fold = make_fit(row_embed, row_square)
    start_fit = jnp.zeros((group_size, epochs_count), jnp.float32)
    col_embed, col_fitted = (
        lax.all_gather(curve_embed, "row", axis=0, tiled=True),
        lax.all_gather(fitted_own, "row", axis=0, tiled=True),
    )
    fitted_sum = fit_fold(start_fit, (col_embed, col_fitted), 0)
    epochs = jnp.arange(epochs_count, dtype=jnp.int32)
    fitted_mine = lax.psum_scatter(fitted_sum, "col", scatter_dimension=0, tiled=True)
    observed = epochs[None, :] < lengths[:, None]
    adjoint_own = jnp.where(observed, targets.astype(jnp.float32) - fitted_mine, 0.0).astype(
        jnp.bfloat16
    )
    adjoint = lax.all_gather(adjoint_own, "col", axis=0, tiled=True)
    grad_fold = make_grad(row_embed, row_square, row_wide, adjoint)
    start_grad = (
        jnp.zeros((group_size, width), jnp.float32),
        jnp.zeros((column_size, width), jnp.float32),
    )
    row_sum, col_sum = grad_fold(start_grad, (col_embed, col_fitted), 0)
    group_base = lax.axis_index("row") * group_size
    local_curve = (row_curve - group_base).astype(jnp.int32)
    inverse = (
        jnp.zeros((group_size,), jnp.int32)
        .at[local_curve]
        .set(jnp.arange(group_size, dtype=jnp.int32))
    )
    reordered = jnp.take(row_sum, inverse, axis=0)
    factor = 2.0 / width
    row_grad = lax.psum_scatter(reordered, "col", scatter_dimension=0, tiled=True) * factor
    col_grad = lax.psum_scatter(col_sum, "row", scatter_dimension=0, tiled=True) * factor
    return (row_grad, col_grad)


def power_of_two(number):
    return number >= 2 and number & (number - 1) == 0


def per_device(curve_embed, solution, *rest):
    own, width = curve_embed.shape
    rows_axis, cols_axis = lax.axis_size("row"), lax.axis_size("col")
    gathered = own * rows_axis * cols_axis * (width + solution.shape[1]) * 2
    if gathered <= GATHER_LIMIT and rows_axis >= 8 and own <= solution.shape[1] and power_of_two(rows_axis) and cols_axis == 4:
        return gathered_plan(curve_embed, solution, *rest)
    return tiled_plan(curve_embed, solution, *rest)


def solution(mesh):
    in_specs = (
        P(("row", "col"), None),
        P(("row", "col"), None),
        P(("row", "col"), None),
        P(("row", "col")),
        P(("row", "col")),
        P(),
    )
    out_specs = (P(("row", "col"), None), P(("row", "col"), None))
    return jax.shard_map(
        per_device, mesh=mesh, in_specs=in_specs, out_specs=out_specs, check_vma=False
    )
```
